512 devices in a mesh: group: 8 (over y, core), box: 64 (over z, x).
Axes of the slice: x: 4, y: 4, z: 16, core: 2. Of those that a mesh axis runs over, the one named last changes fastest.
Arguments:
- old_state: float32 [2, 9, 32, 1024, 128], P(None, None, 'group', 'box'), may hold values from -6 to 6
- owners: int32 [8, 2, 64], P('group'), may hold values from 0 to 63, as said below
- diffusivity: bfloat16 [9, 32, 1024, 128], P(None, 'group', 'box'), may hold values from 0.25 to 4
Outputs:
- smoothed: float32 [9, 32, 1024, 128], P(None, 'group', 'box')
The draws below stay inside these ranges and needn't reach their ends.
Inputs may be any that keep to these rules, and one draw needn't show every extreme that they name: owners[g, 0, j] is the index along the cluster of the device that holds box j before the regrid and owners[g, 1, j] its slot (0 or 1). The old owner lies in the same aligned block of 4 boxes as j; no two boxes share an owner and a slot; in the first block of every cluster one device holds two boxes and some box's old owner differs from it in both of the two lowest bits of the index.
All inputs are finite; a program needn't handle non-finite values.
Results may differ from the reference program's by a relative error of at most 0.0003.
Values may be sent and summed in bfloat16 or wider, within the bound.
A program may use at most 64 MiB of HBM per device.

```python
import math
import jax
import jax.numpy as jnp
from jax import lax

SPECIES = 9
CX = 4
CZ = 16
CY = 128
ITERS = 4
SLOTS = 2
BLOCK = 4
CLUSTERS = 8
BOXES = 64
NX = 32
NZ = 1024


def draw_owners(key, part):
    key = jax.random.fold_in(key, 11)
    subkeys = jax.random.split(key, 3)
    block_count = CLUSTERS * BOXES // BLOCK
    box_order = jax.vmap(lambda subkey: jax.random.permutation(subkey, BLOCK))(jax.random.split(subkeys[0], block_count))
    owner_order = jax.vmap(lambda subkey: jax.random.permutation(subkey, BLOCK))(jax.random.split(subkeys[1], block_count))
    doubled = jax.random.randint(subkeys[2], (block_count,), 0, 2)
    leading = jnp.arange(block_count) % (BOXES // BLOCK) == 0
    doubled = jnp.where(leading, 1, doubled)
    owner_order = jnp.where(leading[:, None], jnp.bitwise_xor(box_order, BLOCK - 1), owner_order)
    rank_owner = owner_order.at[:, 1].set(jnp.where(doubled == 1, owner_order[:, 0], owner_order[:, 1]))
    rank_slot = jnp.zeros_like(owner_order).at[:, 1].set(doubled)
    inverse = jnp.argsort(box_order, axis=1)
    holder = jnp.take_along_axis(rank_owner, inverse, axis=1)
    slot_of = jnp.take_along_axis(rank_slot, inverse, axis=1)
    block_start = jnp.arange(block_count) % (BOXES // BLOCK) * BLOCK
    holder = holder + block_start[:, None]
    return jnp.stack([holder.reshape(CLUSTERS, BOXES), slot_of.reshape(CLUSTERS, BOXES)], axis=1).astype(jnp.int32)


def block_levels(key, shape, pieces, smallest, largest):
    def one(position, parts):
        heights = jax.random.uniform(jax.random.fold_in(jax.random.fold_in(key, 6), position), (parts,), jnp.float32, smallest / len(pieces), largest / len(pieces))
        return jnp.repeat(jnp.exp(heights), shape[position] // parts).reshape((-1,) + (1,) * (len(shape) - position - 1))

    loudness = one(*pieces[0])
    for cut in pieces[1:]:
        loudness = loudness * one(*cut)
    return loudness


def bell_draw(own_key, extent, spread, most, shards=(), kind=jnp.bfloat16):
    values = jax.random.normal(own_key, extent, jnp.float32) * spread
    if len(shards) > 0:
        values = block_levels(own_key, extent, shards, -0.22, 0.18) * values
    return jnp.clip(values, min=-most, max=most).astype(kind)


def setup_inputs(seed: int = 0) -> dict:
    key_of = jax.random.split(jax.random.key(seed), 4)
    return {
        "old_state": bell_draw(key_of[0], (SLOTS, SPECIES, NX, NZ, CY), 1.0, 6.0, ((2, 8), (3, 64)), jnp.float32),
        "owners": draw_owners(jax.random.fold_in(key_of[3], 71), 0),
        "diffusivity": jnp.clip(jnp.exp(math.log(4.0) - 2.7725887 * jax.random.uniform(key_of[2], (SPECIES, NX, NZ, CY), jnp.float32) ** block_levels(key_of[2], (SPECIES, NX, NZ, CY), ((1, 8), (2, 64)), -0.2, 0.2)), 0.25, 4.0).astype(jnp.bfloat16),
    }


relax_weight = 0.5


def interior(array):
    return array[..., 1:-1, 1:-1, :]


def face_terms(padded):
    center = interior(padded)
    return (0.5 * (center + padded[..., :-2, 1:-1, :]),
            0.5 * (center + padded[..., 2:, 1:-1, :]),
            0.5 * (center + padded[..., 1:-1, :-2, :]),
            0.5 * (center + padded[..., 1:-1, 2:, :]),
            0.5 * (center + jnp.roll(center, 1, axis=-1)),
            0.5 * (center + jnp.roll(center, -1, axis=-1)))


def neighbour_sum(beside_all, face_set):
    center = interior(beside_all)
    total = face_set[0] * beside_all[..., :-2, 1:-1, :] + face_set[1] * beside_all[..., 2:, 1:-1, :]
    total = total + face_set[2] * beside_all[..., 1:-1, :-2, :] + face_set[3] * beside_all[..., 1:-1, 2:, :]
    total = total + face_set[4] * jnp.roll(center, 1, axis=-1) + face_set[5] * jnp.roll(center, -1, axis=-1)
    return total


def relax_step(beside_all, source, face_set, diagonal):
    return (source + relax_weight * neighbour_sum(beside_all, face_set)) / diagonal


def diagonal_of(face_set):
    return 1.0 + relax_weight * (face_set[0] + face_set[1] + face_set[2] + face_set[3] + face_set[4] + face_set[5])


def reference(old_state, owners, diffusivity):
    holder = owners[:, 0, :]
    slot_of = owners[:, 1, :]
    cluster = jnp.arange(CLUSTERS, dtype=jnp.int32)[:, None]

    def one_species(species_id):
        species_plane = lax.dynamic_index_in_dim(old_state, species_id, 1, keepdims=False)
        blocks = species_plane.reshape(SLOTS, CLUSTERS, CX, BOXES, CZ, CY)
        picked = blocks[slot_of, cluster, :, holder]
        regridded = jnp.transpose(picked, (0, 2, 1, 3, 4)).reshape(NX, NZ, CY)
        coefficient = lax.dynamic_index_in_dim(diffusivity, species_id, 0, keepdims=False).astype(jnp.float32)
        padded = jnp.pad(coefficient, ((1, 1), (1, 1), (0, 0)))
        face_set = face_terms(padded)
        diagonal = diagonal_of(face_set)
        current = regridded
        for repeat in range(ITERS):
            beside_all = jnp.pad(current, ((1, 1), (1, 1), (0, 0)))
            current = relax_step(beside_all, regridded, face_set, diagonal)
        return current

    return lax.map(one_species, jnp.arange(SPECIES, dtype=jnp.int32))
```

```python
import functools

import jax
import jax.numpy as jnp
from jax import lax
from jax.experimental import pallas as pl
from jax.experimental.pallas import tpu as pltpu
from jax.sharding import PartitionSpec as P

MESH = pl.DeviceIdType.MESH
BLOCK = 4
ITERS = 4
LEVELS = 32767.0
ZROWS = 24


def low_rows():
    return lax.broadcasted_iota(jnp.int32, (8, 128), 0) < 4


def pack_edges(rows):
    low = low_rows()
    first, last = [], []
    for a in (0, 2):
        p, q = rows[a], rows[a + 1]
        first.append(jnp.where(low, p[0:8], pltpu.roll(q[0:8], 4, 0)))
        last.append(jnp.where(low, pltpu.roll(p[8:16], 4, 0), q[8:16]))
    return jnp.concatenate(first, 0), jnp.concatenate(last, 0)


def unpack_edges(after, before):
    low = low_rows()
    out = []
    for a in range(4):
        n = after[8 * (a // 2):8 * (a // 2) + 8]
        p = before[8 * (a // 2):8 * (a // 2) + 8]
        if a % 2 == 0:
            out.append(jnp.where(low, n, pltpu.roll(p, 4, 0)))
        else:
            out.append(jnp.where(low, pltpu.roll(n, 4, 0), p))
    return out


def kernel(chunks, own_ref, old_ref, dif_ref, out_ref, old, enc, cand, recv, box, beside, edge, got_edge, corner,
           scl, scl_cand, scl_recv, scl_own, scl_got, dif, dif_edge, dif_beside, dif_got, dif_corner,
           coef, slab, cur, wts, res, sem_in, sem_out, sem_dif_in,
           s_send, s_recv, r_send, r_recv, h_send, h_recv, d_send, d_recv, n_send, n_recv):
    species = dif_ref.shape[0]
    g, b = lax.axis_index("group"), lax.axis_index("box")
    groups, boxes = lax.axis_size("group"), lax.axis_size("box")
    x = lax.rem(b, BLOCK)
    base = b - x
    ring = [None] + [(g, base + lax.rem(x + d, BLOCK)) for d in range(1, BLOCK)]
    gs = (lax.rem(g + groups - 1, groups), lax.rem(g + 1, groups))
    bs = (lax.rem(b + 1, boxes), lax.rem(b + boxes - 1, boxes))
    sides = [(gs[0], b), (gs[1], b)]
    ends = [(g, bs[0]), (g, bs[1])]
    diagonal = [[(gs[i], bs[j]) for j in range(2)] for i in range(2)]
    partners = ring[1:] + sides + ends + diagonal[0] + diagonal[1]

    loads = []
    for k, (s0, n) in enumerate(chunks):
        cp = pltpu.make_async_copy(old_ref.at[:, pl.ds(s0, n)], old[k], sem_in.at[k])
        cp.start()
        loads.append(cp)
    dif_load = pltpu.make_async_copy(dif_ref, dif, sem_dif_in)
    dif_load.start()

    barrier = pltpu.get_barrier_semaphore()
    for dev in partners:
        pl.semaphore_signal(barrier, inc=1, device_id=dev, device_id_type=MESH)

    def remote(src, dst, send, recv_sem, dev):
        return pltpu.make_async_remote_copy(src_ref=src, dst_ref=dst, send_sem=send, recv_sem=recv_sem,
                                            device_id=dev, device_id_type=MESH)

    slot = [own_ref[0, 1, base + lax.rem(x + d, BLOCK)] for d in range(BLOCK)]
    holder = own_ref[0, 0, b]
    came = lax.rem(lax.rem(holder, BLOCK) + BLOCK - x, BLOCK)

    dif_load.wait()

    def dif_pack(s, _):
        first, last = pack_edges([dif[s, a].astype(jnp.float32) for a in range(4)])
        dif_edge[0, s] = first.astype(jnp.bfloat16)
        dif_edge[1, s] = last.astype(jnp.bfloat16)
        return 0

    lax.fori_loop(0, species, dif_pack, 0)

    for cp in loads:
        cp.wait()
    for k, (s0, n) in enumerate(chunks):
        for t in range(2):
            for s in range(n):
                m = jnp.max(jnp.abs(old[k][t, s]), axis=0)
                m = jnp.max(m, axis=0, keepdims=True)
                scl[t, pl.ds(s0 + s, 1)] = jnp.maximum(m, 1e-30) * (1.0 / LEVELS)
    for d in range(1, BLOCK):
        scl_cand[d - 1] = scl[slot[d]]
    scl_recv[0] = scl[slot[0]]

    pl.semaphore_wait(barrier, len(partners))

    sends = []
    waits = {}

    def send(name, src, dst, send_sem, recv_sem, dev):
        cp = remote(src, dst, send_sem, recv_sem, dev)
        cp.start()
        sends.append(cp)
        waits.setdefault(name, []).append(cp)

    def arrive(name):
        for cp in waits.pop(name):
            cp.wait_recv()

    for e in range(2):
        send("dif_edge", dif_edge.at[e], dif_got.at[e], d_send.at[e], d_recv.at[e], ends[1 - e])
    for d in range(1, BLOCK):
        send("scl", scl_cand.at[d - 1], scl_recv.at[BLOCK - d], s_send.at[d - 1], s_recv.at[d - 1], ring[d])

    for k, (s0, n) in enumerate(chunks):

        def encode(s, _):
            for t in range(2):
                inv = 1.0 / scl[t, pl.ds(s0 + s, 1)]
                for a in range(4):
                    q = jnp.round(old[k][t, s, a] * inv).astype(jnp.int32)
                    enc[k][t, s, pl.ds(16 * a, 16)] = q.astype(jnp.int16)
            return 0

        lax.fori_loop(0, n, encode, 0)
        for d in range(BLOCK):
            if d:
                cand[k][d - 1] = enc[k][slot[d]]
                send(("regrid", k), cand[k].at[d - 1], recv[k].at[BLOCK - d], r_send.at[k, d - 1], r_recv.at[k, d - 1],
                     ring[d])
            else:
                recv[k][0] = enc[k][slot[0]]
    for i in range(2):
        send("dif_side", dif, dif_beside.at[i], d_send.at[2 + i], d_recv.at[2 + i], sides[1 - i])

    arrive("scl")
    scl_own[...] = scl_recv[came]
    for i in range(2):
        send("scl_all", scl_own, scl_got.at[i, 0], n_send.at[i], n_recv.at[i], sides[1 - i])
        send("scl_all", scl_own, scl_got.at[2, 1 + i], n_send.at[2 + i], n_recv.at[2 + i], ends[1 - i])
        for j in range(2):
            m = 4 + 2 * i + j
            send("scl_all", scl_own, scl_got.at[i, 1 + j], n_send.at[m], n_recv.at[m], diagonal[1 - i][1 - j])

    arrive("dif_edge")
    for i in range(2):
        send("dif_corner", dif_got, dif_corner.at[i], d_send.at[4 + i], d_recv.at[4 + i], sides[1 - i])

    for k, (s0, n) in enumerate(chunks):
        arrive(("regrid", k))

        def choose(s, _):
            q = recv[k][came, s]
            box[k][s] = q
            first, last = pack_edges([q[16 * a:16 * a + 16].astype(jnp.int32) for a in range(4)])
            edge[k][0, s] = first.astype(jnp.int16)
            edge[k][1, s] = last.astype(jnp.int16)
            return 0

        lax.fori_loop(0, n, choose, 0)
        for i in range(2):
            send(("halo", k), box[k], beside[k].at[i], h_send.at[k, i], h_recv.at[k, i], sides[1 - i])
        for e in range(2):
            send(("halo", k), edge[k].at[e], got_edge[k].at[e], h_send.at[k, 2 + e], h_recv.at[k, 2 + e], ends[1 - e])
        for i in range(2):
            for e in range(2):
                m = 4 + 2 * i + e
                send(("halo", k), edge[k].at[e], corner[k].at[i, e], h_send.at[k, m], h_recv.at[k, m],
                     diagonal[1 - i][1 - e])

    in_side = [(g > 0).astype(jnp.float32), (g < groups - 1).astype(jnp.float32)]
    in_end = [(b < boxes - 1).astype(jnp.float32), (b > 0).astype(jnp.float32)]
    row = lax.broadcasted_iota(jnp.int32, (ZROWS, 128), 0)
    in_rows = jnp.where(row < 16, 1.0, jnp.where(row < 20, in_end[0], in_end[1]))

    arrive("dif_side")
    arrive("dif_corner")

    def weigh(s, _):
        for part in range(3):
            for a in range(4):
                rows = dif[s, a] if part == 1 else dif_beside[0 if part == 0 else 1, s, a]
                rows = rows.astype(jnp.float32)
                if part != 1:
                    rows = rows * in_side[0 if part == 0 else 1]
                coef[4 * part + a, 0:16] = rows
            if part == 1:
                after, before = dif_got[0, s], dif_got[1, s]
                m = 1.0
            else:
                i = 0 if part == 0 else 1
                after, before = dif_corner[i, 0, s], dif_corner[i, 1, s]
                m = in_side[i]
            halo = unpack_edges(after.astype(jnp.float32) * (in_end[0] * m), before.astype(jnp.float32) * (in_end[1] * m))
            for a in range(4):
                coef[4 * part + a, 16:24] = halo[a]
        for a in range(1, 11):
            c = coef[a]
            faces = [c + coef[a - 1], c + coef[a + 1],
                     c + pltpu.roll(c, 1, 0), c + pltpu.roll(c, ZROWS - 1, 0),
                     c + pltpu.roll(c, 1, 1), c + pltpu.roll(c, 127, 1)]
            total = (faces[0] + faces[1]) + (faces[2] + faces[3]) + (faces[4] + faces[5])
            scale = in_rows / (1.0 + 0.25 * total)
            if a < 4:
                scale = scale * in_side[0]
            elif a > 7:
                scale = scale * in_side[1]
            wts[s, a - 1, 6] = scale
            scale = 0.25 * scale
            for f in range(6):
                wts[s, a - 1, f] = faces[f] * scale
        return 0

    lax.fori_loop(0, species, weigh, 0)
    arrive("scl_all")

    outs = []
    for k, (s0, n) in enumerate(chunks):
        arrive(("halo", k))

        def smooth(s, _):
            at = s0 + s
            for part in range(3):
                if part == 1:
                    q, after, before = box[k][s], got_edge[k][0, s], got_edge[k][1, s]
                    own_s, after_s, before_s = scl_own[pl.ds(at, 1)], scl_got[2, 1, pl.ds(at, 1)], scl_got[2, 2, pl.ds(at, 1)]
                    m = 1.0
                else:
                    i = 0 if part == 0 else 1
                    q, after, before = beside[k][i, s], corner[k][i, 0, s], corner[k][i, 1, s]
                    own_s, after_s, before_s = (scl_got[i, j, pl.ds(at, 1)] for j in range(3))
                    m = in_side[i]
                    own_s = own_s * m
                q = q.astype(jnp.int32).astype(jnp.float32) * own_s
                after = after.astype(jnp.int32).astype(jnp.float32) * (after_s * (in_end[0] * m))
                before = before.astype(jnp.int32).astype(jnp.float32) * (before_s * (in_end[1] * m))
                halo = unpack_edges(after, before)
                for a in range(4):
                    slab[4 * part + a, 0:16] = q[16 * a:16 * a + 16]
                    slab[4 * part + a, 16:24] = halo[a]
            for it in range(ITERS):
                src = slab if it == 0 else cur.at[(it - 1) % 2]
                for a in range(1 + it, 11 - it):
                    v = src[a]
                    own = slab[a] if it else v
                    w = [wts[at, a - 1, f] for f in range(7)]
                    acc = w[6] * own + w[0] * src[a - 1] + w[1] * src[a + 1]
                    acc = acc + w[2] * pltpu.roll(v, 1, 0) + w[3] * pltpu.roll(v, ZROWS - 1, 0)
                    acc = acc + w[4] * pltpu.roll(v, 1, 1) + w[5] * pltpu.roll(v, 127, 1)
                    if it == ITERS - 1:
                        res[at, a - 4] = acc[0:16]
                    else:
                        cur[it % 2, a] = acc
            return 0

        lax.fori_loop(0, n, smooth, 0)
        cp = pltpu.make_async_copy(res.at[pl.ds(s0, n)], out_ref.at[pl.ds(s0, n)], sem_out.at[k])
        cp.start()
        outs.append(cp)
    for cp in sends:
        cp.wait_send()
    for cp in outs:
        cp.wait()


def cut(species):
    if species >= 9:
        sizes = [3, 3, species - 6]
    else:
        sizes = [1] * species
    chunks, s0 = [], 0
    for n in sizes:
        chunks.append((s0, n))
        s0 += n
    return chunks


def local(old_state, owners, diffusivity):
    species = diffusivity.shape[0]
    chunks = cut(species)
    i16, bf16, f32 = jnp.int16, jnp.bfloat16, jnp.float32
    dma = pltpu.SemaphoreType.DMA
    nk = len(chunks)
    scratch = [
        [pltpu.VMEM((2, n, 4, 16, 128), f32) for _, n in chunks],
        [pltpu.VMEM((2, n, 64, 128), i16) for _, n in chunks],
        [pltpu.VMEM((3, n, 64, 128), i16) for _, n in chunks],
        [pltpu.VMEM((4, n, 64, 128), i16) for _, n in chunks],
        [pltpu.VMEM((n, 64, 128), i16) for _, n in chunks],
        [pltpu.VMEM((2, n, 64, 128), i16) for _, n in chunks],
        [pltpu.VMEM((2, n, 16, 128), i16) for _, n in chunks],
        [pltpu.VMEM((2, n, 16, 128), i16) for _, n in chunks],
        [pltpu.VMEM((2, 2, n, 16, 128), i16) for _, n in chunks],
        pltpu.VMEM((2, species, 128), f32),
        pltpu.VMEM((3, species, 128), f32),
        pltpu.VMEM((4, species, 128), f32),
        pltpu.VMEM((species, 128), f32),
        pltpu.VMEM((3, 3, species, 128), f32),
        pltpu.VMEM((species, 4, 16, 128), bf16),
        pltpu.VMEM((2, species, 16, 128), bf16),
        pltpu.VMEM((2, species, 4, 16, 128), bf16),
        pltpu.VMEM((2, species, 16, 128), bf16),
        pltpu.VMEM((2, 2, species, 16, 128), bf16),
        pltpu.VMEM((12, ZROWS, 128), f32),
        pltpu.VMEM((12, ZROWS, 128), f32),
        pltpu.VMEM((2, 12, ZROWS, 128), f32),
        pltpu.VMEM((species, 10, 7, ZROWS, 128), f32),
        pltpu.VMEM((species, 4, 16, 128), f32),
        dma((nk,)), dma((nk,)), dma(()),
        dma((3,)), dma((3,)), dma((nk, 3)), dma((nk, 3)), dma((nk, 8)), dma((nk, 8)),
        dma((6,)), dma((6,)), dma((8,)), dma((8,)),
    ]
    return pl.pallas_call(
        functools.partial(kernel, chunks),
        out_shape=jax.ShapeDtypeStruct(diffusivity.shape, f32),
        in_specs=[pl.BlockSpec(memory_space=pltpu.SMEM), pl.BlockSpec(memory_space=pl.ANY),
                  pl.BlockSpec(memory_space=pl.ANY)],
        out_specs=pl.BlockSpec(memory_space=pl.ANY),
        scratch_shapes=scratch,
        name="regrid_smooth",
        compiler_params=pltpu.CompilerParams(collective_id=0, has_side_effects=True, vmem_limit_bytes=40 * 2**20),
    )(owners, old_state, diffusivity)


def solution(mesh):
    placed = (
        P(None, None, "group", "box", None),
        P("group", None, None),
        P(None, "group", "box", None),
    )
    return jax.shard_map(
        local, mesh=mesh, in_specs=placed, out_specs=P(None, "group", "box", None), check_vma=False
    )
```

```python
import functools

import jax
import jax.numpy as jnp
from jax import lax
from jax.experimental import pallas as pl
from jax.experimental.pallas import tpu as pltpu
from jax.sharding import PartitionSpec as P

MESH = pl.DeviceIdType.MESH
BLOCK = 4
ITERS = 4
LEVELS = 32767.0
ZROWS = 24


def when(condition, act):
    if condition is None:
        act()
    else:
        pl.when(condition)(act)


def low_rows():
    return lax.broadcasted_iota(jnp.int32, (8, 128), 0) < 4


def pack_edges(rows):
    low = low_rows()
    first, last = [], []
    for a in (0, 2):
        p, q = rows[a], rows[a + 1]
        first.append(jnp.where(low, p[0:8], pltpu.roll(q[0:8], 4, 0)))
        last.append(jnp.where(low, pltpu.roll(p[8:16], 4, 0), q[8:16]))
    return jnp.concatenate(first, 0), jnp.concatenate(last, 0)


def unpack_edges(after, before):
    low = low_rows()
    out = []
    for a in range(4):
        n = after[8 * (a // 2):8 * (a // 2) + 8]
        p = before[8 * (a // 2):8 * (a // 2) + 8]
        if a % 2 == 0:
            out.append(jnp.where(low, n, pltpu.roll(p, 4, 0)))
        else:
            out.append(jnp.where(low, pltpu.roll(n, 4, 0), p))
    return out


def kernel(chunks, own_hbm, old_ref, dif_ref, res, own_ref, old, enc, cand, recv, box, beside, edge, got_edge, corner,
           scl, scl_cand, scl_recv, scl_own, scl_got, dif, dif_edge, dif_beside, dif_got, dif_corner,
           coef, slab, cur, wts, sem_in, sem_dif_in,
           s_send, s_recv, r_send, r_recv, h_send, h_recv, d_send, d_recv, n_send, n_recv):
    species = dif_ref.shape[0]
    g, b = lax.axis_index("group"), lax.axis_index("box")
    groups, boxes = lax.axis_size("group"), lax.axis_size("box")
    x = lax.rem(b, BLOCK)
    base = b - x
    ring = [None] + [(g, base + lax.rem(x + d, BLOCK)) for d in range(1, BLOCK)]
    gs = (lax.rem(g + groups - 1, groups), lax.rem(g + 1, groups))
    bs = (lax.rem(b + 1, boxes), lax.rem(b + boxes - 1, boxes))
    sides = [(gs[0], b), (gs[1], b)]
    ends = [(g, bs[0]), (g, bs[1])]
    diagonal = [[(gs[i], bs[j]) for j in range(2)] for i in range(2)]
    has_side = [g > 0, g < groups - 1]
    has_end = [b < boxes - 1, b > 0]
    around = [(sides[i], has_side[i]) for i in range(2)] + [(ends[j], has_end[j]) for j in range(2)]
    around += [(diagonal[i][j], jnp.logical_and(has_side[i], has_end[j])) for i in range(2) for j in range(2)]

    own_load = pltpu.make_async_copy(own_hbm, own_ref, sem_dif_in.at[1])
    own_load.start()
    loads = []
    for k, (s0, n) in enumerate(chunks):
        cp = pltpu.make_async_copy(old_ref.at[:, pl.ds(s0, n)], old[k], sem_in.at[k])
        cp.start()
        loads.append(cp)
    dif_load = pltpu.make_async_copy(dif_ref, dif, sem_dif_in.at[0])
    dif_load.start()

    barrier = pltpu.get_barrier_semaphore()
    for dev in ring[1:]:
        pl.semaphore_signal(barrier, inc=1, device_id=dev, device_id_type=MESH)
    for dev, there in around:

        @pl.when(there)
        def _():
            pl.semaphore_signal(barrier, inc=1, device_id=dev, device_id_type=MESH)

    def remote(src, dst, send, recv_sem, dev):
        return pltpu.make_async_remote_copy(src_ref=src, dst_ref=dst, send_sem=send, recv_sem=recv_sem,
                                            device_id=dev, device_id_type=MESH)

    own_load.wait()
    slot = [own_ref[0, 1, base + lax.rem(x + d, BLOCK)] for d in range(BLOCK)]
    holder = own_ref[0, 0, b]
    came = lax.rem(lax.rem(holder, BLOCK) + BLOCK - x, BLOCK)

    dif_load.wait()

    def dif_pack(s, _):
        first, last = pack_edges([dif[s, a].astype(jnp.float32) for a in range(4)])
        dif_edge[0, s] = first.astype(jnp.bfloat16)
        dif_edge[1, s] = last.astype(jnp.bfloat16)
        return 0

    lax.fori_loop(0, species, dif_pack, 0)

    for cp in loads:
        cp.wait()
    for k, (s0, n) in enumerate(chunks):
        for t in range(2):
            for s in range(n):
                m = jnp.max(jnp.abs(old[k][t, s]), axis=0)
                m = jnp.max(m, axis=0, keepdims=True)
                scl[t, pl.ds(s0 + s, 1)] = jnp.maximum(m, 1e-30) * (1.0 / LEVELS)
    for d in range(1, BLOCK):
        scl_cand[d - 1] = scl[slot[d]]
    scl_recv[0] = scl[slot[0]]

    in_sides = has_side[0].astype(jnp.int32) + has_side[1].astype(jnp.int32)
    in_ends = has_end[0].astype(jnp.int32) + has_end[1].astype(jnp.int32)
    pl.semaphore_wait(barrier, BLOCK - 1 + in_sides + in_ends + in_sides * in_ends)

    sends = []
    waits = {}

    def send(name, src, dst, send_sem, recv_sem, dev, to=None, come=None):
        cp = remote(src, dst, send_sem, recv_sem, dev)
        when(to, cp.start)
        sends.append((cp, to))
        waits.setdefault(name, []).append((cp, come))

    def arrive(name):
        for cp, come in waits.pop(name):
            when(come, cp.wait_recv)

    def send_side(name, src, dst, send_sem, recv_sem, i):
        send(name, src, dst, send_sem, recv_sem, sides[1 - i], has_side[1 - i], has_side[i])

    def send_end(name, src, dst, send_sem, recv_sem, j):
        send(name, src, dst, send_sem, recv_sem, ends[1 - j], has_end[1 - j], has_end[j])

    def send_diagonal(name, src, dst, send_sem, recv_sem, i, j):
        send(name, src, dst, send_sem, recv_sem, diagonal[1 - i][1 - j],
             jnp.logical_and(has_side[1 - i], has_end[1 - j]), jnp.logical_and(has_side[i], has_end[j]))

    for e in range(2):
        send_end("dif_edge", dif_edge.at[e], dif_got.at[e], d_send.at[e], d_recv.at[e], e)
    for d in range(1, BLOCK):
        send("scl", scl_cand.at[d - 1], scl_recv.at[BLOCK - d], s_send.at[d - 1], s_recv.at[d - 1], ring[d])

    for k, (s0, n) in enumerate(chunks):

        def encode(s, _):
            for t in range(2):
                inv = 1.0 / scl[t, pl.ds(s0 + s, 1)]
                for a in range(4):
                    q = jnp.round(old[k][t, s, a] * inv).astype(jnp.int32)
                    enc[k][t, s, pl.ds(16 * a, 16)] = q.astype(jnp.int16)
            return 0

        lax.fori_loop(0, n, encode, 0)
        for d in range(BLOCK):
            if d:
                cand[k][d - 1] = enc[k][slot[d]]
                send(("regrid", k), cand[k].at[d - 1], recv[k].at[BLOCK - d], r_send.at[k, d - 1], r_recv.at[k, d - 1],
                     ring[d])
            else:
                recv[k][0] = enc[k][slot[0]]
    for i in range(2):
        send_side("dif_side", dif, dif_beside.at[i], d_send.at[2 + i], d_recv.at[2 + i], i)

    arrive("scl")
    scl_own[...] = scl_recv[came]
    for i in range(2):
        send_side("scl_all", scl_own, scl_got.at[i, 0], n_send.at[i], n_recv.at[i], i)
        send_end("scl_all", scl_own, scl_got.at[2, 1 + i], n_send.at[2 + i], n_recv.at[2 + i], i)
        for j in range(2):
            m = 4 + 2 * i + j
            send_diagonal("scl_all", scl_own, scl_got.at[i, 1 + j], n_send.at[m], n_recv.at[m], i, j)

    arrive("dif_edge")
    for i in range(2):
        send_side("dif_corner", dif_got, dif_corner.at[i], d_send.at[4 + i], d_recv.at[4 + i], i)

    for k, (s0, n) in enumerate(chunks):
        arrive(("regrid", k))

        def choose(s, _):
            q = recv[k][came, s]
            box[k][s] = q
            first, last = pack_edges([q[16 * a:16 * a + 16].astype(jnp.int32) for a in range(4)])
            edge[k][0, s] = first.astype(jnp.int16)
            edge[k][1, s] = last.astype(jnp.int16)
            return 0

        lax.fori_loop(0, n, choose, 0)
        for i in range(2):
            send_side(("halo", k), box[k], beside[k].at[i], h_send.at[k, i], h_recv.at[k, i], i)
        for e in range(2):
            send_end(("halo", k), edge[k].at[e], got_edge[k].at[e], h_send.at[k, 2 + e], h_recv.at[k, 2 + e], e)
        for i in range(2):
            for e in range(2):
                m = 4 + 2 * i + e
                send_diagonal(("halo", k), edge[k].at[e], corner[k].at[i, e], h_send.at[k, m], h_recv.at[k, m], i, e)

    in_side = [there.astype(jnp.float32) for there in has_side]
    in_end = [there.astype(jnp.float32) for there in has_end]

    def kept(there, value):
        return jnp.where(there, value, 0.0)

    def both(i, j):
        return has_end[j] if i is None else jnp.logical_and(has_side[i], has_end[j])

    row = lax.broadcasted_iota(jnp.int32, (ZROWS, 128), 0)
    in_rows = jnp.where(row < 16, 1.0, jnp.where(row < 20, in_end[0], in_end[1]))

    arrive("dif_side")
    arrive("dif_corner")

    def weigh(s, _):
        for part, i in ((0, 0), (1, None), (2, 1)):
            for a in range(4):
                if i is None:
                    coef[4 * part + a, 0:16] = dif[s, a].astype(jnp.float32)
                else:
                    coef[4 * part + a, 0:16] = kept(has_side[i], dif_beside[i, s, a].astype(jnp.float32))
            tiles = [dif_got[j, s] if i is None else dif_corner[i, j, s] for j in range(2)]
            halo = unpack_edges(*[kept(both(i, j), tiles[j].astype(jnp.float32)) for j in range(2)])
            for a in range(4):
                coef[4 * part + a, 16:24] = halo[a]
        for a in range(1, 11):
            c = coef[a]
            faces = [c + coef[a - 1], c + coef[a + 1],
                     c + pltpu.roll(c, 1, 0), c + pltpu.roll(c, ZROWS - 1, 0),
                     c + pltpu.roll(c, 1, 1), c + pltpu.roll(c, 127, 1)]
            total = (faces[0] + faces[1]) + (faces[2] + faces[3]) + (faces[4] + faces[5])
            scale = in_rows / (1.0 + 0.25 * total)
            if a < 4:
                scale = scale * in_side[0]
            elif a > 7:
                scale = scale * in_side[1]
            wts[s, a - 1, 6] = scale
            scale = 0.25 * scale
            for f in range(6):
                wts[s, a - 1, f] = faces[f] * scale
        return 0

    lax.fori_loop(0, species, weigh, 0)
    arrive("scl_all")

    for k, (s0, n) in enumerate(chunks):
        arrive(("halo", k))

        def smooth(s, _):
            at = s0 + s
            for part, i in ((0, 0), (1, None), (2, 1)):
                if i is None:
                    q = box[k][s].astype(jnp.int32).astype(jnp.float32) * scl_own[pl.ds(at, 1)]
                    tiles = [got_edge[k][j, s] for j in range(2)]
                    scales = [scl_got[2, 1 + j, pl.ds(at, 1)] for j in range(2)]
                else:
                    q = beside[k][i, s].astype(jnp.int32).astype(jnp.float32)
                    q = q * kept(has_side[i], scl_got[i, 0, pl.ds(at, 1)])
                    tiles = [corner[k][i, j, s] for j in range(2)]
                    scales = [scl_got[i, 1 + j, pl.ds(at, 1)] for j in range(2)]
                halo = unpack_edges(*[tiles[j].astype(jnp.int32).astype(jnp.float32) * kept(both(i, j), scales[j])
                                      for j in range(2)])
                for a in range(4):
                    slab[4 * part + a, 0:16] = q[16 * a:16 * a + 16]
                    slab[4 * part + a, 16:24] = halo[a]
            for it in range(ITERS):
                src = slab if it == 0 else cur.at[(it - 1) % 2]
                for a in range(1 + it, 11 - it):
                    v = src[a]
                    own = slab[a] if it else v
                    w = [wts[at, a - 1, f] for f in range(7)]
                    acc = w[6] * own + w[0] * src[a - 1] + w[1] * src[a + 1]
                    acc = acc + w[2] * pltpu.roll(v, 1, 0) + w[3] * pltpu.roll(v, ZROWS - 1, 0)
                    acc = acc + w[4] * pltpu.roll(v, 1, 1) + w[5] * pltpu.roll(v, 127, 1)
                    if it == ITERS - 1:
                        res[at, a - 4] = acc[0:16]
                    else:
                        cur[it % 2, a] = acc
            return 0

        lax.fori_loop(0, n, smooth, 0)
    for cp, to in sends:
        when(to, cp.wait_send)


def cut(species):
    if species >= 9:
        sizes = [3, 3, species - 6]
    else:
        sizes = [1] * species
    chunks, s0 = [], 0
    for n in sizes:
        chunks.append((s0, n))
        s0 += n
    return chunks


def local(old_state, owners, diffusivity):
    species = diffusivity.shape[0]
    chunks = cut(species)
    i16, bf16, f32 = jnp.int16, jnp.bfloat16, jnp.float32
    dma = pltpu.SemaphoreType.DMA
    nk = len(chunks)
    scratch = [
        pltpu.SMEM(owners.shape, jnp.int32),
        [pltpu.VMEM((2, n, 4, 16, 128), f32) for _, n in chunks],
        [pltpu.VMEM((2, n, 64, 128), i16) for _, n in chunks],
        [pltpu.VMEM((3, n, 64, 128), i16) for _, n in chunks],
        [pltpu.VMEM((4, n, 64, 128), i16) for _, n in chunks],
        [pltpu.VMEM((n, 64, 128), i16) for _, n in chunks],
        [pltpu.VMEM((2, n, 64, 128), i16) for _, n in chunks],
        [pltpu.VMEM((2, n, 16, 128), i16) for _, n in chunks],
        [pltpu.VMEM((2, n, 16, 128), i16) for _, n in chunks],
        [pltpu.VMEM((2, 2, n, 16, 128), i16) for _, n in chunks],
        pltpu.VMEM((2, species, 128), f32),
        pltpu.VMEM((3, species, 128), f32),
        pltpu.VMEM((4, species, 128), f32),
        pltpu.VMEM((species, 128), f32),
        pltpu.VMEM((3, 3, species, 128), f32),
        pltpu.VMEM((species, 4, 16, 128), bf16),
        pltpu.VMEM((2, species, 16, 128), bf16),
        pltpu.VMEM((2, species, 4, 16, 128), bf16),
        pltpu.VMEM((2, species, 16, 128), bf16),
        pltpu.VMEM((2, 2, species, 16, 128), bf16),
        pltpu.VMEM((12, ZROWS, 128), f32),
        pltpu.VMEM((12, ZROWS, 128), f32),
        pltpu.VMEM((2, 12, ZROWS, 128), f32),
        pltpu.VMEM((species, 10, 7, ZROWS, 128), f32),
        dma((nk,)), dma((2,)),
        dma((3,)), dma((3,)), dma((nk, 3)), dma((nk, 3)), dma((nk, 8)), dma((nk, 8)),
        dma((6,)), dma((6,)), dma((8,)), dma((8,)),
    ]
    old_state, owners, diffusivity = (
        pltpu.with_memory_space_constraint(v, pltpu.HBM) for v in (old_state, owners, diffusivity)
    )
    return pl.pallas_call(
        functools.partial(kernel, chunks),
        out_shape=pltpu.VMEM(diffusivity.shape, f32),
        in_specs=[pl.BlockSpec(memory_space=pltpu.HBM)] * 3,
        out_specs=pl.BlockSpec(memory_space=pltpu.VMEM),
        scratch_shapes=scratch,
        name="regrid_smooth",
        compiler_params=pltpu.CompilerParams(collective_id=0, has_side_effects=True, vmem_limit_bytes=40 * 2**20),
    )(owners, old_state, diffusivity)


def solution(mesh):
    placed = (
        P(None, None, "group", "box", None),
        P("group", None, None),
        P(None, "group", "box", None),
    )
    return jax.shard_map(
        local, mesh=mesh, in_specs=placed, out_specs=P(None, "group", "box", None), check_vma=False
    )
```

```python
import functools

import jax
import jax.numpy as jnp
from jax import lax
from jax.experimental import pallas as pl
from jax.experimental.pallas import tpu as pltpu
from jax.sharding import PartitionSpec as P

MESH = pl.DeviceIdType.MESH
BLOCK = 4
ITERS = 4
LEVELS = 32767.0
ZROWS = 24


def when(condition, act):
    if condition is None:
        act()
    else:
        pl.when(condition)(act)


def low_rows():
    return lax.broadcasted_iota(jnp.int32, (8, 128), 0) < 4


def pack_edges(rows):
    low = low_rows()
    first, last = [], []
    for a in (0, 2):
        p, q = rows[a], rows[a + 1]
        first.append(jnp.where(low, p[0:8], pltpu.roll(q[0:8], 4, 0)))
        last.append(jnp.where(low, pltpu.roll(p[8:16], 4, 0), q[8:16]))
    return jnp.concatenate(first, 0), jnp.concatenate(last, 0)


def unpack_edges(after, before):
    low = low_rows()
    out = []
    for a in range(4):
        n = after[8 * (a // 2):8 * (a // 2) + 8]
        p = before[8 * (a // 2):8 * (a // 2) + 8]
        if a % 2 == 0:
            out.append(jnp.where(low, n, pltpu.roll(p, 4, 0)))
        else:
            out.append(jnp.where(low, pltpu.roll(n, 4, 0), p))
    return out


def pack_tips(first, last):
    row = lax.broadcasted_iota(jnp.int32, (8, 128), 0)
    f01, f23, l01, l23 = first[0:8], first[8:16], last[0:8], last[8:16]
    return (
        (jnp.where(row == 7, pltpu.roll(f01, 3, 0), f23), jnp.where(row == 3, pltpu.roll(f23, 3, 0), f01)),
        (jnp.where(row == 4, pltpu.roll(l01, 5, 0), l23), jnp.where(row == 0, pltpu.roll(l23, 5, 0), l01)),
    )


def unpack_tips(side, n, p):
    low = low_rows()
    if side == 0:
        return {
            3: jnp.where(low, pltpu.roll(n, 4, 0), p),
            2: jnp.where(low, n, pltpu.roll(p, 4, 0)),
            1: jnp.where(low, pltpu.roll(n, 1, 0), pltpu.roll(p, 3, 0)),
        }
    return {
        0: jnp.where(low, n, pltpu.roll(p, 4, 0)),
        1: jnp.where(low, pltpu.roll(n, 4, 0), p),
        2: jnp.where(low, pltpu.roll(n, 5, 0), pltpu.roll(p, 7, 0)),
    }


def kernel(chunks, own_hbm, old_ref, dif_ref, res, own_ref, old, enc, far, near, mix, merged, recv, box, beside, edge, got_edge, tips, tip,
           corner, corner_f32,
           scl, scl_cand, scl_recv, scl_own, scl_got, dif, dif_edge, dif_beside, dif_got, dif_corner,
           coef, slab, cur, wts, sem_in, sem_dif_in,
           s_send, s_recv, f_send, f_recv, r_send, r_recv, h_send, h_recv, d_send, d_recv, n_send, n_recv):
    species = dif_ref.shape[0]
    g, b = lax.axis_index("group"), lax.axis_index("box")
    groups, boxes = lax.axis_size("group"), lax.axis_size("box")
    x = lax.rem(b, BLOCK)
    base = b - x
    ring = [None] + [(g, base + lax.rem(x + d, BLOCK)) for d in range(1, BLOCK)]
    gs = (lax.rem(g + groups - 1, groups), lax.rem(g + 1, groups))
    bs = (lax.rem(b + 1, boxes), lax.rem(b + boxes - 1, boxes))
    sides = [(gs[0], b), (gs[1], b)]
    ends = [(g, bs[0]), (g, bs[1])]
    diagonal = [[(gs[i], bs[j]) for j in range(2)] for i in range(2)]
    has_side = [g > 0, g < groups - 1]
    has_end = [b < boxes - 1, b > 0]
    around = [(sides[i], has_side[i]) for i in range(2)] + [(ends[j], has_end[j]) for j in range(2)]
    around += [(diagonal[i][j], jnp.logical_and(has_side[i], has_end[j])) for i in range(2) for j in range(2)]

    own_load = pltpu.make_async_copy(own_hbm, own_ref, sem_dif_in.at[1])
    own_load.start()
    loads = []
    for k, (s0, n) in enumerate(chunks):
        cp = pltpu.make_async_copy(old_ref.at[:, pl.ds(s0, n)], old[k], sem_in.at[k])
        cp.start()
        loads.append(cp)
    dif_load = pltpu.make_async_copy(dif_ref, dif, sem_dif_in.at[0])
    dif_load.start()

    barrier = pltpu.get_barrier_semaphore()
    for dev in ring[1:]:
        pl.semaphore_signal(barrier, inc=1, device_id=dev, device_id_type=MESH)
    for dev, there in around:

        @pl.when(there)
        def _():
            pl.semaphore_signal(barrier, inc=1, device_id=dev, device_id_type=MESH)

    def remote(src, dst, send, recv_sem, dev):
        return pltpu.make_async_remote_copy(src_ref=src, dst_ref=dst, send_sem=send, recv_sem=recv_sem,
                                            device_id=dev, device_id_type=MESH)

    own_load.wait()
    slot = [own_ref[0, 1, base + lax.rem(x + d, BLOCK)] for d in range(BLOCK)]
    holder = own_ref[0, 0, b]
    came = lax.rem(lax.rem(holder, BLOCK) + BLOCK - x, BLOCK)
    left, right = lax.rem(x + BLOCK - 1, BLOCK), lax.rem(x + 1, BLOCK)
    behind = (lax.rem(own_ref[0, 0, base + left], BLOCK) == right, lax.rem(own_ref[0, 0, base + right], BLOCK) == left)
    place = [jnp.where(came == 0, 0, jnp.where(came == (3, 1)[h], 2, 1)) for h in range(2)]

    for cp in loads:
        cp.wait()
    for k, (s0, n) in enumerate(chunks):
        for t in range(2):
            for s in range(n):
                m = jnp.max(jnp.abs(old[k][t, s]), axis=0)
                m = jnp.max(m, axis=0, keepdims=True)
                scl[t, pl.ds(s0 + s, 1)] = jnp.maximum(m, 1e-30) * (1.0 / LEVELS)
    for d in range(1, BLOCK):
        scl_cand[d - 1] = scl[slot[d]]
    scl_recv[0] = scl[slot[0]]

    for k, (s0, n) in enumerate(chunks):

        def encode(s, _):
            for t in range(2):
                inv = 1.0 / scl[t, pl.ds(s0 + s, 1)]
                for a in range(4):
                    q = jnp.round(old[k][t, s, a] * inv).astype(jnp.int32)
                    enc[k][t, a // 2, s, pl.ds(16 * (a % 2), 16)] = q.astype(jnp.int16)
            return 0

        lax.fori_loop(0, n, encode, 0)
        for h in range(2):
            far[k][h] = enc[k][slot[2], h]
            near[k][h] = enc[k][slot[(1, 3)[h]], h]
            mix[k][h][1] = enc[k][slot[(3, 1)[h]], h]
            recv[k][h][0] = enc[k][slot[0], h]
    dif_load.wait()

    in_sides = has_side[0].astype(jnp.int32) + has_side[1].astype(jnp.int32)
    in_ends = has_end[0].astype(jnp.int32) + has_end[1].astype(jnp.int32)
    pl.semaphore_wait(barrier, BLOCK - 1 + in_sides + in_ends + in_sides * in_ends)

    sends = []
    waits = {}

    def send(name, src, dst, send_sem, recv_sem, dev, to=None, come=None):
        cp = remote(src, dst, send_sem, recv_sem, dev)
        when(to, cp.start)
        sends.append((cp, to))
        waits.setdefault(name, []).append((cp, come))

    def arrive(name):
        for cp, come in waits.pop(name):
            when(come, cp.wait_recv)

    def send_side(name, src, dst, send_sem, recv_sem, i):
        send(name, src, dst, send_sem, recv_sem, sides[1 - i], has_side[1 - i], has_side[i])

    def send_end(name, src, dst, send_sem, recv_sem, j):
        send(name, src, dst, send_sem, recv_sem, ends[1 - j], has_end[1 - j], has_end[j])

    def send_diagonal(name, src, dst, send_sem, recv_sem, i, j):
        send(name, src, dst, send_sem, recv_sem, diagonal[1 - i][1 - j],
             jnp.logical_and(has_side[1 - i], has_end[1 - j]), jnp.logical_and(has_side[i], has_end[j]))

    for k in range(len(chunks)):
        for h in range(2):
            send(("far", k), far[k].at[h], mix[k][h].at[0], f_send.at[k, h], f_recv.at[k, h], ring[(BLOCK - 1, 1)[h]])
    for d in range(1, BLOCK):
        send("scl", scl_cand.at[d - 1], scl_recv.at[BLOCK - d], s_send.at[d - 1], s_recv.at[d - 1], ring[d])
    for k in range(len(chunks)):
        for h in range(2):
            send(("regrid", k), near[k].at[h], recv[k][h].at[2], r_send.at[k, h], r_recv.at[k, h],
                 ring[(1, BLOCK - 1)[h]])
    for i in range(2):
        send_side("dif_side", dif, dif_beside.at[i], d_send.at[2 + i], d_recv.at[2 + i], i)


    def dif_pack(s, _):
        first, last = pack_edges([dif[s, a].astype(jnp.float32) for a in range(4)])
        dif_edge[0, s] = first.astype(jnp.bfloat16)
        dif_edge[1, s] = last.astype(jnp.bfloat16)
        return 0

    lax.fori_loop(0, species, dif_pack, 0)

    for e in range(2):
        send_end("dif_edge", dif_edge.at[e], dif_got.at[e], d_send.at[e], d_recv.at[e], e)

    for k in range(len(chunks)):
        arrive(("far", k))
        for h in range(2):
            merged[k][h] = mix[k][h][jnp.where(behind[h], 0, 1)]
            send(("regrid", k), merged[k].at[h], recv[k][h].at[1], r_send.at[k, 2 + h], r_recv.at[k, 2 + h],
                 ring[(BLOCK - 1, 1)[h]])

    arrive("scl")
    scl_own[...] = scl_recv[came]
    for i in range(2):
        send_side("scl_all", scl_own, scl_got.at[i, 0], n_send.at[i], n_recv.at[i], i)
        send_end("scl_all", scl_own, scl_got.at[2, 1 + i], n_send.at[2 + i], n_recv.at[2 + i], i)
        for j in range(2):
            m = 4 + 2 * i + j
            send_diagonal("scl_all", scl_own, scl_got.at[i, 1 + j], n_send.at[m], n_recv.at[m], i, j)

    arrive("dif_edge")
    for i in range(2):
        send_side("dif_corner", dif_got, dif_corner.at[i], d_send.at[4 + i], d_recv.at[4 + i], i)

    for k, (s0, n) in enumerate(chunks):
        arrive(("regrid", k))

        def choose(s, _):
            layers = []
            for h in range(2):
                q = recv[k][h][place[h], s]
                box[k][s, pl.ds(32 * h, 32)] = q
                q = q.astype(jnp.int32)
                layers += [q[0:16], q[16:32]]
            first, last = pack_edges(layers)
            edge[k][0, s] = first.astype(jnp.int16)
            edge[k][1, s] = last.astype(jnp.int16)
            tip_rows = pack_tips(first, last)
            for e in range(2):
                for i in range(2):
                    tips[k][i, e, s] = tip_rows[e][i]
            return 0

        lax.fori_loop(0, n, choose, 0)
        for i in range(2):
            for e in range(2):
                for m in range(tip[k].shape[2]):
                    pair = tips[k][i, e, pl.ds(2 * m, 2)].reshape(16, 128)
                    tip[k][i, e, m] = pair.astype(jnp.int16)
        for i in range(2):
            send_side(("halo", k), box[k], beside[k].at[i], h_send.at[k, i], h_recv.at[k, i], i)
        for e in range(2):
            send_end(("halo", k), edge[k].at[e], got_edge[k].at[e], h_send.at[k, 2 + e], h_recv.at[k, 2 + e], e)
        for i in range(2):
            for e in range(2):
                m = 4 + 2 * i + e
                send_diagonal(("halo", k), tip[k].at[i, e], corner[k].at[i, e], h_send.at[k, m], h_recv.at[k, m], i, e)

    in_side = [there.astype(jnp.float32) for there in has_side]
    in_end = [there.astype(jnp.float32) for there in has_end]

    def kept(there, value):
        return jnp.where(there, value, 0.0)

    def both(i, j):
        return has_end[j] if i is None else jnp.logical_and(has_side[i], has_end[j])

    row = lax.broadcasted_iota(jnp.int32, (ZROWS, 128), 0)
    in_rows = jnp.where(row < 16, 1.0, jnp.where(row < 20, in_end[0], in_end[1]))

    arrive("dif_side")
    arrive("dif_corner")

    def weigh(s, _):
        for part, i in ((0, 0), (1, None), (2, 1)):
            for a in range(4):
                if i is None:
                    coef[4 * part + a, 0:16] = dif[s, a].astype(jnp.float32)
                else:
                    coef[4 * part + a, 0:16] = kept(has_side[i], dif_beside[i, s, a].astype(jnp.float32))
            tiles = [dif_got[j, s] if i is None else dif_corner[i, j, s] for j in range(2)]
            halo = unpack_edges(*[kept(both(i, j), tiles[j].astype(jnp.float32)) for j in range(2)])
            for a in range(4):
                coef[4 * part + a, 16:24] = halo[a]
        for a in range(1, 11):
            c = coef[a]
            faces = [c + coef[a - 1], c + coef[a + 1],
                     c + pltpu.roll(c, 1, 0), c + pltpu.roll(c, ZROWS - 1, 0),
                     c + pltpu.roll(c, 1, 1), c + pltpu.roll(c, 127, 1)]
            total = (faces[0] + faces[1]) + (faces[2] + faces[3]) + (faces[4] + faces[5])
            scale = in_rows / (1.0 + 0.25 * total)
            if a < 4:
                scale = scale * in_side[0]
            elif a > 7:
                scale = scale * in_side[1]
            wts[s, a - 1, 6] = scale
            scale = 0.25 * scale
            for f in range(6):
                wts[s, a - 1, f] = faces[f] * scale
        return 0

    lax.fori_loop(0, species, weigh, 0)
    arrive("scl_all")

    for k, (s0, n) in enumerate(chunks):
        arrive(("halo", k))
        for i in range(2):
            for e in range(2):
                for m in range(tip[k].shape[2]):
                    pair = corner[k][i, e, m].astype(jnp.int32).astype(jnp.float32)
                    corner_f32[i, e, pl.ds(2 * m, 2)] = pair.reshape(2, 8, 128)

        def smooth(s, _):
            at = s0 + s
            for part, i in ((0, 0), (1, None), (2, 1)):
                if i is None:
                    q = box[k][s].astype(jnp.int32).astype(jnp.float32) * scl_own[pl.ds(at, 1)]
                    halo = dict(enumerate(unpack_edges(*[
                        got_edge[k][j, s].astype(jnp.int32).astype(jnp.float32)
                        * kept(has_end[j], scl_got[2, 1 + j, pl.ds(at, 1)]) for j in range(2)])))
                else:
                    q = beside[k][i, s].astype(jnp.int32).astype(jnp.float32)
                    q = q * kept(has_side[i], scl_got[i, 0, pl.ds(at, 1)])
                    halo = unpack_tips(i, *[corner_f32[i, j, s] * kept(both(i, j), scl_got[i, 1 + j, pl.ds(at, 1)])
                                            for j in range(2)])
                for a in range(4):
                    slab[4 * part + a, 0:16] = q[16 * a:16 * a + 16]
                    if a in halo:
                        slab[4 * part + a, 16:24] = halo[a]
            for it in range(ITERS):
                src = slab if it == 0 else cur.at[(it - 1) % 2]
                for a in range(1 + it, 11 - it):
                    v = src[a]
                    own = slab[a] if it else v
                    w = [wts[at, a - 1, f] for f in range(7)]
                    acc = w[6] * own + w[0] * src[a - 1] + w[1] * src[a + 1]
                    acc = acc + w[2] * pltpu.roll(v, 1, 0) + w[3] * pltpu.roll(v, ZROWS - 1, 0)
                    acc = acc + w[4] * pltpu.roll(v, 1, 1) + w[5] * pltpu.roll(v, 127, 1)
                    if it == ITERS - 1:
                        res[at, a - 4] = acc[0:16]
                    else:
                        cur[it % 2, a] = acc
            return 0

        lax.fori_loop(0, n, smooth, 0)
    for cp, to in sends:
        when(to, cp.wait_send)


def cut(species):
    if species >= 9:
        sizes = [3, 3, species - 6]
    else:
        sizes = [1] * species
    chunks, s0 = [], 0
    for n in sizes:
        chunks.append((s0, n))
        s0 += n
    return chunks


def local(old_state, owners, diffusivity):
    species = diffusivity.shape[0]
    chunks = cut(species)
    i16, bf16, f32 = jnp.int16, jnp.bfloat16, jnp.float32
    dma = pltpu.SemaphoreType.DMA
    nk = len(chunks)
    scratch = [
        pltpu.SMEM(owners.shape, jnp.int32),
        [pltpu.VMEM((2, n, 4, 16, 128), f32) for _, n in chunks],
        [pltpu.VMEM((2, 2, n, 32, 128), i16) for _, n in chunks],
        [pltpu.VMEM((2, n, 32, 128), i16) for _, n in chunks],
        [pltpu.VMEM((2, n, 32, 128), i16) for _, n in chunks],
        [[pltpu.VMEM((2, n, 32, 128), i16) for _ in range(2)] for _, n in chunks],
        [pltpu.VMEM((2, n, 32, 128), i16) for _, n in chunks],
        [[pltpu.VMEM((3, n, 32, 128), i16) for _ in range(2)] for _, n in chunks],
        [pltpu.VMEM((n, 64, 128), i16) for _, n in chunks],
        [pltpu.VMEM((2, n, 64, 128), i16) for _, n in chunks],
        [pltpu.VMEM((2, n, 16, 128), i16) for _, n in chunks],
        [pltpu.VMEM((2, n, 16, 128), i16) for _, n in chunks],
        [pltpu.VMEM((2, 2, n + n % 2, 8, 128), jnp.int32) for _, n in chunks],
        [pltpu.VMEM((2, 2, (n + 1) // 2, 16, 128), i16) for _, n in chunks],
        [pltpu.VMEM((2, 2, (n + 1) // 2, 16, 128), i16) for _, n in chunks],
        pltpu.VMEM((2, 2, max(n for _, n in chunks) + 1, 8, 128), f32),
        pltpu.VMEM((2, species, 128), f32),
        pltpu.VMEM((3, species, 128), f32),
        pltpu.VMEM((4, species, 128), f32),
        pltpu.VMEM((species, 128), f32),
        pltpu.VMEM((3, 3, species, 128), f32),
        pltpu.VMEM((species, 4, 16, 128), bf16),
        pltpu.VMEM((2, species, 16, 128), bf16),
        pltpu.VMEM((2, species, 4, 16, 128), bf16),
        pltpu.VMEM((2, species, 16, 128), bf16),
        pltpu.VMEM((2, 2, species, 16, 128), bf16),
        pltpu.VMEM((12, ZROWS, 128), f32),
        pltpu.VMEM((12, ZROWS, 128), f32),
        pltpu.VMEM((2, 12, ZROWS, 128), f32),
        pltpu.VMEM((species, 10, 7, ZROWS, 128), f32),
        dma((nk,)), dma((2,)),
        dma((3,)), dma((3,)), dma((nk, 2)), dma((nk, 2)), dma((nk, 4)), dma((nk, 4)), dma((nk, 8)), dma((nk, 8)),
        dma((6,)), dma((6,)), dma((8,)), dma((8,)),
    ]
    old_state, owners, diffusivity = (
        pltpu.with_memory_space_constraint(v, pltpu.HBM) for v in (old_state, owners, diffusivity)
    )
    return pl.pallas_call(
        functools.partial(kernel, chunks),
        out_shape=pltpu.VMEM(diffusivity.shape, f32),
        in_specs=[pl.BlockSpec(memory_space=pltpu.HBM)] * 3,
        out_specs=pl.BlockSpec(memory_space=pltpu.VMEM),
        scratch_shapes=scratch,
        name="regrid_smooth",
        compiler_params=pltpu.CompilerParams(collective_id=0, has_side_effects=True, vmem_limit_bytes=40 * 2**20),
    )(owners, old_state, diffusivity)


def solution(mesh):
    placed = (
        P(None, None, "group", "box", None),
        P("group", None, None),
        P(None, "group", "box", None),
    )
    return jax.shard_map(
        local, mesh=mesh, in_specs=placed, out_specs=P(None, "group", "box", None), check_vma=False
    )
```

```python
import jax
import jax.numpy as jnp
from jax import lax
from jax.experimental import pallas as pl
from jax.experimental.pallas import tpu as pltpu
from jax.sharding import PartitionSpec as P

MESH = pl.DeviceIdType.MESH
BLOCK = 4
ITERS = 4
LEVELS = 32767.0
ZROWS = 24


def when(condition, act):
    if condition is None:
        act()
    else:
        pl.when(condition)(act)


def low_rows():
    return lax.broadcasted_iota(jnp.int32, (8, 128), 0) < 4


def pack_edges(rows):
    low = low_rows()
    first, last = [], []
    for a in (0, 2):
        p, q = rows[a], rows[a + 1]
        first.append(jnp.where(low, p[0:8], pltpu.roll(q[0:8], 4, 0)))
        last.append(jnp.where(low, pltpu.roll(p[8:16], 4, 0), q[8:16]))
    return jnp.concatenate(first, 0), jnp.concatenate(last, 0)


def unpack_edges(after, before):
    low = low_rows()
    out = []
    for a in range(4):
        n = after[8 * (a // 2):8 * (a // 2) + 8]
        p = before[8 * (a // 2):8 * (a // 2) + 8]
        if a % 2 == 0:
            out.append(jnp.where(low, n, pltpu.roll(p, 4, 0)))
        else:
            out.append(jnp.where(low, pltpu.roll(n, 4, 0), p))
    return out


def pack_tips(first, last):
    row = lax.broadcasted_iota(jnp.int32, (8, 128), 0)
    f01, f23, l01, l23 = first[0:8], first[8:16], last[0:8], last[8:16]
    return (
        (jnp.where(row == 7, pltpu.roll(f01, 3, 0), f23), jnp.where(row == 3, pltpu.roll(f23, 3, 0), f01)),
        (jnp.where(row == 4, pltpu.roll(l01, 5, 0), l23), jnp.where(row == 0, pltpu.roll(l23, 5, 0), l01)),
    )


def unpack_tips(side, n, p):
    low = low_rows()
    if side == 0:
        return {
            3: jnp.where(low, pltpu.roll(n, 4, 0), p),
            2: jnp.where(low, n, pltpu.roll(p, 4, 0)),
            1: jnp.where(low, pltpu.roll(n, 1, 0), pltpu.roll(p, 3, 0)),
        }
    return {
        0: jnp.where(low, n, pltpu.roll(p, 4, 0)),
        1: jnp.where(low, pltpu.roll(n, 4, 0), p),
        2: jnp.where(low, pltpu.roll(n, 5, 0), pltpu.roll(p, 7, 0)),
    }


def kernel(own_hbm, old_ref, dif_ref, res, own_ref, old, far, via, near, mine, merged, got, kept_own, box, beside,
           edge, got_edge, tips, tip, corner, corner_f32, scl_cand, scl_recv, scl_own, scl_got,
           dif, dif_edge, dif_beside, dif_got, dif_corner, coef, slab, cur, wts, pool,
           sem_in, sem_out, sem_far, sem_regrid, sem_halo, sem_scl, sem_dif):
    species = dif_ref.shape[0]
    count, size, pairs = tip.shape[0], slab.shape[0], tip.shape[3]
    g, b = lax.axis_index("group"), lax.axis_index("box")
    groups, boxes = lax.axis_size("group"), lax.axis_size("box")
    x = lax.rem(b, BLOCK)
    base = b - x
    ring = [None] + [(g, base + lax.rem(x + d, BLOCK)) for d in range(1, BLOCK)]
    gs = (lax.rem(g + groups - 1, groups), lax.rem(g + 1, groups))
    bs = (lax.rem(b + 1, boxes), lax.rem(b + boxes - 1, boxes))
    sides = [(gs[0], b), (gs[1], b)]
    ends = [(g, bs[0]), (g, bs[1])]
    diagonal = [[(gs[i], bs[j]) for j in range(2)] for i in range(2)]
    has_side = [g > 0, g < groups - 1]
    has_end = [b < boxes - 1, b > 0]

    def both(i, j):
        return has_end[j] if i is None else jnp.logical_and(has_side[i], has_end[j])

    around = [(sides[i], has_side[i]) for i in range(2)] + [(ends[j], has_end[j]) for j in range(2)]
    around += [(diagonal[i][j], both(i, j)) for i in range(2) for j in range(2)]

    barrier = pltpu.get_barrier_semaphore()
    for dev in ring[1:]:
        pl.semaphore_signal(barrier, inc=1, device_id=dev, device_id_type=MESH)
    for dev, there in around:

        @pl.when(there)
        def _():
            pl.semaphore_signal(barrier, inc=1, device_id=dev, device_id_type=MESH)

    old_load = pltpu.make_async_copy(old_ref, old, sem_in.at[0])
    old_load.start()
    own_load = pltpu.make_async_copy(own_hbm, own_ref, sem_in.at[1])
    own_load.start()
    dif_load = pltpu.make_async_copy(dif_ref, dif, sem_in.at[2])
    dif_load.start()

    def message(src, dst, recv_sem, dev, to=None):
        cp = pltpu.make_async_remote_copy(src_ref=src, dst_ref=dst, send_sem=sem_out, recv_sem=recv_sem,
                                          device_id=dev, device_id_type=MESH)
        return cp, to

    def to_side(src, dst, recv_sem, i):
        return message(src, dst, recv_sem, sides[1 - i], has_side[1 - i])

    def to_end(src, dst, recv_sem, j):
        return message(src, dst, recv_sem, ends[1 - j], has_end[1 - j])

    def to_diagonal(src, dst, recv_sem, i, j):
        return message(src, dst, recv_sem, diagonal[1 - i][1 - j], both(1 - i, 1 - j))

    def start(messages):
        for cp, to in messages:
            when(to, cp.start)

    def wait_units(sem, units):
        span = pool.at[pl.ds(0, 8 * units)]
        pltpu.make_async_copy(span, span, sem).wait()

    in_sides = has_side[0].astype(jnp.int32) + has_side[1].astype(jnp.int32)
    in_ends = has_end[0].astype(jnp.int32) + has_end[1].astype(jnp.int32)

    def wait_around(sem, units):
        for ns in (1, 2):
            for ne in (1, 2):

                @pl.when(jnp.logical_and(in_sides == ns, in_ends == ne))
                def _():
                    wait_units(sem, units(ns, ne))

    scl_units = scl_own.shape[0] // 8

    def halo_units(ns, ne):
        return ne * size + ns * ne * pairs + ns * 4 * size

    def all_units(ns, ne):
        fixed = 3 * 4 * species + 3 * scl_units
        around = scl_units * (ns + ne + ns * ne) + species * (6 * ns + ne)
        return fixed + around + count * halo_units(ns, ne)

    def part(k):
        return pl.ds(k * size, size)

    ahead = (ring[BLOCK - 1], ring[1])

    def far_messages(k):
        return [message(far.at[h, part(k)], via.at[h, part(k)], sem_far.at[k], ahead[h]) for h in range(2)]

    def near_messages(k):
        return [message(near.at[h, part(k)], got.at[1, h, part(k)], sem_regrid.at[k], ahead[1 - h]) for h in range(2)]

    def merged_messages(k):
        return [message(merged.at[h, part(k)], got.at[0, h, part(k)], sem_regrid.at[k], ahead[h]) for h in range(2)]

    def halo_messages(k):
        out = [to_end(edge.at[e, part(k)], got_edge.at[e, part(k)], sem_halo.at[k], e) for e in range(2)]
        out += [to_diagonal(tip.at[k, i, e], corner.at[k, i, e], sem_halo.at[k], i, e)
                for i in range(2) for e in range(2)]
        return out + [to_side(box.at[part(k)], beside.at[i, part(k)], sem_halo.at[k], i) for i in range(2)]

    scl_messages = [message(scl_cand.at[d - 1], scl_recv.at[BLOCK - d], sem_scl.at[0], ring[d]) for d in range(1, BLOCK)]
    scl_around = [to_side(scl_own, scl_got.at[i, 0], sem_scl.at[1], i) for i in range(2)]
    scl_around += [to_end(scl_own, scl_got.at[2, 1 + j], sem_scl.at[1], j) for j in range(2)]
    scl_around += [to_diagonal(scl_own, scl_got.at[i, 1 + j], sem_scl.at[1], i, j) for i in range(2) for j in range(2)]
    dif_ends = [to_end(dif_edge.at[e], dif_got.at[e], sem_dif.at[0], e) for e in range(2)]
    dif_sides = [to_side(dif, dif_beside.at[i], sem_dif.at[1], i) for i in range(2)]
    dif_corners = [to_side(dif_got, dif_corner.at[i], sem_dif.at[1], i) for i in range(2)]

    def each(n, act):
        def body(k, _):
            act(k)
            return 0

        lax.fori_loop(0, n, body, 0)

    own_load.wait()
    first_slot = [own_ref[0, 1, base + lax.rem(x + d, BLOCK)] == 0 for d in range(BLOCK)]
    holder = own_ref[0, 0, b]
    came = lax.rem(lax.rem(holder, BLOCK) + BLOCK - x, BLOCK)
    left, right = lax.rem(x + BLOCK - 1, BLOCK), lax.rem(x + 1, BLOCK)
    behind = (lax.rem(own_ref[0, 0, base + left], BLOCK) == right, lax.rem(own_ref[0, 0, base + right], BLOCK) == left)
    old_load.wait()

    def encode(s):
        codes, scales = [], []
        for t in range(2):
            layers = [old[t, s, a] for a in range(4)]
            m = jnp.maximum(jnp.maximum(jnp.abs(layers[0]), jnp.abs(layers[1])),
                            jnp.maximum(jnp.abs(layers[2]), jnp.abs(layers[3])))
            m = jnp.maximum(jnp.max(m, axis=0, keepdims=True), 1e-30)
            scale = m * (1.0 / LEVELS)
            inv = 1.0 / scale
            rows = [jnp.round(v * inv).astype(jnp.int32) for v in layers]
            codes.append([jnp.concatenate(rows[2 * h:2 * h + 2], 0) for h in range(2)])
            scales.append(scale)

        def code(d, h):
            return jnp.where(first_slot[d], codes[0][h], codes[1][h]).astype(jnp.int16)

        for h in range(2):
            far[h, s] = code(2, h)
            near[h, s] = code((1, 3)[h], h)
            mine[h, s] = code((3, 1)[h], h)
            kept_own[h, s] = code(0, h)
        for d in range(BLOCK):
            scale = jnp.where(first_slot[d], scales[0], scales[1])
            if d:
                scl_cand[d - 1, pl.ds(s, 1)] = scale
            else:
                scl_recv[0, pl.ds(s, 1)] = scale

    each(species, encode)
    dif_load.wait()

    pl.semaphore_wait(barrier, BLOCK - 1 + in_sides + in_ends + in_sides * in_ends)

    each(count, lambda k: start(far_messages(k)))
    start(scl_messages)
    each(count, lambda k: start(near_messages(k)))
    start(dif_sides)

    def dif_pack(s):
        first, last = pack_edges([dif[s, a].astype(jnp.float32) for a in range(4)])
        dif_edge[0, s] = first.astype(jnp.bfloat16)
        dif_edge[1, s] = last.astype(jnp.bfloat16)

    each(species, dif_pack)
    start(dif_ends)

    def merge(k):
        wait_units(sem_far.at[k], 4 * size)
        for q in range(size):
            for h in range(2):
                s = k * size + q
                merged[h, s] = jnp.where(behind[h], via[h, s], mine[h, s])
        start(merged_messages(k))

    each(count, merge)

    wait_units(sem_scl.at[0], 3 * scl_units)
    scl_own[...] = scl_recv[came]
    start(scl_around)
    wait_around(sem_dif.at[0], lambda ns, ne: species * ne)
    start(dif_corners)

    def choose(k):
        wait_units(sem_regrid.at[k], 8 * size)
        for c in range(size):
            s = k * size + c
            layers = []
            for h in range(2):
                q = jnp.where(came == 0, kept_own[h, s], jnp.where(came == (3, 1)[h], got[1, h, s], got[0, h, s]))
                box[s, pl.ds(32 * h, 32)] = q
                q = q.astype(jnp.int32)
                layers += [q[0:16], q[16:32]]
            first, last = pack_edges(layers)
            edge[0, s] = first.astype(jnp.int16)
            edge[1, s] = last.astype(jnp.int16)
            tip_rows = pack_tips(first, last)
            for e in range(2):
                for i in range(2):
                    tips[i, e, c] = tip_rows[e][i]
        for i in range(2):
            for e in range(2):
                for m in range(tip.shape[3]):
                    pair = tips[i, e, pl.ds(2 * m, 2)].reshape(16, 128)
                    tip[k, i, e, m] = pair.astype(jnp.int16)
        start(halo_messages(k))

    each(count, choose)

    in_side = [there.astype(jnp.float32) for there in has_side]
    in_end = [there.astype(jnp.float32) for there in has_end]

    def kept(there, value):
        return jnp.where(there, value, 0.0)

    row = lax.broadcasted_iota(jnp.int32, (ZROWS, 128), 0)
    in_rows = jnp.where(row < 16, 1.0, jnp.where(row < 20, in_end[0], in_end[1]))

    wait_around(sem_dif.at[1], lambda ns, ne: 6 * species * ns)

    def weigh(at):
        for block, i in ((0, 0), (1, None), (2, 1)):
            for a in range(4):
                if i is None:
                    coef[4 * block + a, 0:16] = dif[at, a].astype(jnp.float32)
                else:
                    coef[4 * block + a, 0:16] = kept(has_side[i], dif_beside[i, at, a].astype(jnp.float32))
            tiles = [dif_got[j, at] if i is None else dif_corner[i, j, at] for j in range(2)]
            halo = unpack_edges(*[kept(both(i, j), tiles[j].astype(jnp.float32)) for j in range(2)])
            for a in range(4):
                coef[4 * block + a, 16:24] = halo[a]
        c = coef[0]
        from_layer = None
        for a in range(11):
            above = coef[a + 1]
            to_layer = 0.25 * (c + above)
            wts[at, a, 0] = to_layer
            if a:
                to_row = 0.25 * (c + pltpu.roll(c, ZROWS - 1, 0))
                to_column = 0.25 * (c + pltpu.roll(c, 127, 1))
                total = (to_layer + from_layer) + (to_row + pltpu.roll(to_row, 1, 0))
                total = total + (to_column + pltpu.roll(to_column, 1, 1))
                inverse = in_rows / (1.0 + total)
                if a < 4:
                    inverse = inverse * in_side[0]
                elif a > 7:
                    inverse = inverse * in_side[1]
                wts[at, a, 1] = to_row
                wts[at, a, 2] = to_column
                wts[at, a, 3] = inverse
            from_layer, c = to_layer, above

    each(species, weigh)

    wait_around(sem_scl.at[1], lambda ns, ne: scl_units * (ns + ne + ns * ne))

    def smooth(k):
        wait_around(sem_halo.at[k], halo_units)
        for i in range(2):
            for e in range(2):
                for m in range(tip.shape[3]):
                    pair = corner[k, i, e, m].astype(jnp.int32).astype(jnp.float32)
                    corner_f32[i, e, pl.ds(2 * m, 2)] = pair.reshape(2, 8, 128)
        for s in range(size):
            at = k * size + s
            for block, i in ((0, 0), (1, None), (2, 1)):
                if i is None:
                    q = box[at].astype(jnp.int32).astype(jnp.float32) * scl_own[pl.ds(at, 1)]
                    halo = dict(enumerate(unpack_edges(*[
                        got_edge[j, at].astype(jnp.int32).astype(jnp.float32)
                        * kept(has_end[j], scl_got[2, 1 + j, pl.ds(at, 1)]) for j in range(2)])))
                else:
                    q = beside[i, at].astype(jnp.int32).astype(jnp.float32)
                    q = q * kept(has_side[i], scl_got[i, 0, pl.ds(at, 1)])
                    halo = unpack_tips(i, *[corner_f32[i, j, s] * kept(both(i, j), scl_got[i, 1 + j, pl.ds(at, 1)])
                                            for j in range(2)])
                for a in range(4):
                    slab[s, 4 * block + a, 0:16] = q[16 * a:16 * a + 16]
                    if a in halo:
                        slab[s, 4 * block + a, 16:24] = halo[a]
        for it in range(ITERS):
            for s in range(size):
                at = k * size + s
                src = slab.at[s] if it == 0 else cur.at[(it - 1) % 2, s]
                below, v = src[it], src[it + 1]
                from_layer = wts[at, it, 0]
                for a in range(1 + it, 11 - it):
                    rows = 16 if it == ITERS - 1 or a in (1 + it, 10 - it) else ZROWS
                    above = src[a + 1]
                    to_layer, to_row, to_column, inverse = (wts[at, a, f] for f in range(4))
                    acc = slab[s, a] + from_layer * below + to_layer * above
                    acc = acc + (pltpu.roll(to_row * v, 1, 0) + to_row * pltpu.roll(v, ZROWS - 1, 0))
                    v_rows, to_rows = v[0:rows], to_column[0:rows]
                    acc = acc[0:rows] + (pltpu.roll(to_rows * v_rows, 1, 1) + to_rows * pltpu.roll(v_rows, 127, 1))
                    acc = acc * inverse[0:rows]
                    if it == ITERS - 1:
                        res[at, a - 4] = acc
                    else:
                        cur[it % 2, s, a, 0:rows] = acc
                    from_layer, below, v = to_layer, v, above

    each(count, smooth)
    wait_around(sem_out, all_units)


def local(old_state, owners, diffusivity):
    species = diffusivity.shape[0]
    size = 3 if species % 3 == 0 else 1
    count = species // size
    pairs, padded = (size + 1) // 2, (species + 7) // 8 * 8
    units = 18 * species + 3 * padded // 8 + padded + 14 * species + count * (10 * size + 4 * pairs)
    i16, i32, bf16, f32 = jnp.int16, jnp.int32, jnp.bfloat16, jnp.float32
    dma = pltpu.SemaphoreType.DMA
    halves = pltpu.VMEM((2, species, 32, 128), i16)
    scratch = [
        pltpu.SMEM(owners.shape, i32),
        pltpu.VMEM(old_state.shape, f32),
        halves, halves, halves, halves, halves,
        pltpu.VMEM((2, 2, species, 32, 128), i16),
        halves,
        pltpu.VMEM((species, 64, 128), i16),
        pltpu.VMEM((2, species, 64, 128), i16),
        pltpu.VMEM((2, species, 16, 128), i16),
        pltpu.VMEM((2, species, 16, 128), i16),
        pltpu.VMEM((2, 2, 2 * pairs, 8, 128), i32),
        pltpu.VMEM((count, 2, 2, pairs, 16, 128), i16),
        pltpu.VMEM((count, 2, 2, pairs, 16, 128), i16),
        pltpu.VMEM((2, 2, 2 * pairs, 8, 128), f32),
        pltpu.VMEM((3, padded, 128), f32),
        pltpu.VMEM((4, padded, 128), f32),
        pltpu.VMEM((padded, 128), f32),
        pltpu.VMEM((3, 3, padded, 128), f32),
        pltpu.VMEM((species, 4, 16, 128), bf16),
        pltpu.VMEM((2, species, 16, 128), bf16),
        pltpu.VMEM((2, species, 4, 16, 128), bf16),
        pltpu.VMEM((2, species, 16, 128), bf16),
        pltpu.VMEM((2, 2, species, 16, 128), bf16),
        pltpu.VMEM((12, ZROWS, 128), f32),
        pltpu.VMEM((size, 12, ZROWS, 128), f32),
        pltpu.VMEM((2, size, 12, ZROWS, 128), f32),
        pltpu.VMEM((species, 11, 4, ZROWS, 128), f32),
        pltpu.VMEM((8 * units, 128), f32),
        dma((3,)), dma(()), dma((count,)), dma((count,)), dma((count,)), dma((2,)), dma((2,)),
    ]
    old_state, owners, diffusivity = (
        pltpu.with_memory_space_constraint(v, pltpu.HBM) for v in (old_state, owners, diffusivity)
    )
    return pl.pallas_call(
        kernel,
        out_shape=pltpu.VMEM(diffusivity.shape, f32),
        in_specs=[pl.BlockSpec(memory_space=pltpu.HBM)] * 3,
        out_specs=pl.BlockSpec(memory_space=pltpu.VMEM),
        scratch_shapes=scratch,
        name="regrid_smooth",
        compiler_params=pltpu.CompilerParams(collective_id=0, has_side_effects=True, vmem_limit_bytes=40 * 2**20),
    )(owners, old_state, diffusivity)


def solution(mesh):
    placed = (
        P(None, None, "group", "box", None),
        P("group", None, None),
        P(None, "group", "box", None),
    )
    return jax.shard_map(
        local, mesh=mesh, in_specs=placed, out_specs=P(None, "group", "box", None), check_vma=False
    )
```

```python
import jax
import jax.numpy as jnp
from jax import lax
from jax.experimental import pallas as pl
from jax.experimental.pallas import tpu as pltpu
from jax.sharding import PartitionSpec as P

MESH = pl.DeviceIdType.MESH
BLOCK = 4
ITERS = 4
LEVELS = 32767.0
ZROWS = 24


def when(condition, act):
    if condition is None:
        act()
    else:
        pl.when(condition)(act)


def low_rows():
    return lax.broadcasted_iota(jnp.int32, (8, 128), 0) < 4


def pack_edges(rows):
    low = low_rows()
    first, last = [], []
    for a in (0, 2):
        p, q = rows[a], rows[a + 1]
        first.append(jnp.where(low, p[0:8], pltpu.roll(q[0:8], 4, 0)))
        last.append(jnp.where(low, pltpu.roll(p[8:16], 4, 0), q[8:16]))
    return jnp.concatenate(first, 0), jnp.concatenate(last, 0)


def unpack_edges(after, before):
    low = low_rows()
    out = []
    for a in range(4):
        n = after[8 * (a // 2):8 * (a // 2) + 8]
        p = before[8 * (a // 2):8 * (a // 2) + 8]
        if a % 2 == 0:
            out.append(jnp.where(low, n, pltpu.roll(p, 4, 0)))
        else:
            out.append(jnp.where(low, pltpu.roll(n, 4, 0), p))
    return out


def pack_tips(first, last):
    row = lax.broadcasted_iota(jnp.int32, (8, 128), 0)
    f01, f23, l01, l23 = first[0:8], first[8:16], last[0:8], last[8:16]
    return (
        (jnp.where(row == 7, pltpu.roll(f01, 3, 0), f23), jnp.where(row == 3, pltpu.roll(f23, 3, 0), f01)),
        (jnp.where(row == 4, pltpu.roll(l01, 5, 0), l23), jnp.where(row == 0, pltpu.roll(l23, 5, 0), l01)),
    )


def unpack_tips(side, n, p):
    low = low_rows()
    if side == 0:
        return {
            3: jnp.where(low, pltpu.roll(n, 4, 0), p),
            2: jnp.where(low, n, pltpu.roll(p, 4, 0)),
            1: jnp.where(low, pltpu.roll(n, 1, 0), pltpu.roll(p, 3, 0)),
        }
    return {
        0: jnp.where(low, n, pltpu.roll(p, 4, 0)),
        1: jnp.where(low, pltpu.roll(n, 4, 0), p),
        2: jnp.where(low, pltpu.roll(n, 5, 0), pltpu.roll(p, 7, 0)),
    }


def kernel(own_hbm, old_ref, dif_ref, res, own_ref, old, far, via, near, mine, merged, got, kept_own, box, beside,
           edge, got_edge, tips, tip, corner, corner_f32, scl_f32, scl_cand, scl_recv, scl_set, scl_beside, scl,
           dif, dif_edge, dif_beside, dif_got, dif_corner, coef, slab, cur, wts, pool,
           sem_in, sem_out, sem_far, sem_regrid, sem_halo, sem_scl, sem_dif):
    species = dif_ref.shape[0]
    count, size, pairs = tip.shape[0], slab.shape[0], tip.shape[3]
    g, b = lax.axis_index("group"), lax.axis_index("box")
    groups, boxes = lax.axis_size("group"), lax.axis_size("box")
    x = lax.rem(b, BLOCK)
    base = b - x
    ring = [None] + [(g, base + lax.rem(x + d, BLOCK)) for d in range(1, BLOCK)]
    gs = (lax.rem(g + groups - 1, groups), lax.rem(g + 1, groups))
    bs = (lax.rem(b + 1, boxes), lax.rem(b + boxes - 1, boxes))
    sides = [(gs[0], b), (gs[1], b)]
    ends = [(g, bs[0]), (g, bs[1])]
    diagonal = [[(gs[i], bs[j]) for j in range(2)] for i in range(2)]
    has_side = [g > 0, g < groups - 1]
    has_end = [b < boxes - 1, b > 0]

    def both(i, j):
        return has_end[j] if i is None else jnp.logical_and(has_side[i], has_end[j])

    around = [(sides[i], has_side[i]) for i in range(2)] + [(ends[j], has_end[j]) for j in range(2)]
    around += [(diagonal[i][j], both(i, j)) for i in range(2) for j in range(2)]

    barrier = pltpu.get_barrier_semaphore()
    for dev in ring[1:]:
        pl.semaphore_signal(barrier, inc=1, device_id=dev, device_id_type=MESH)
    for dev, there in around:

        @pl.when(there)
        def _():
            pl.semaphore_signal(barrier, inc=1, device_id=dev, device_id_type=MESH)

    old_load = pltpu.make_async_copy(old_ref, old, sem_in.at[0])
    old_load.start()
    own_load = pltpu.make_async_copy(own_hbm, own_ref, sem_in.at[1])
    own_load.start()
    dif_load = pltpu.make_async_copy(dif_ref, dif, sem_in.at[2])
    dif_load.start()

    def message(src, dst, recv_sem, dev, to=None):
        cp = pltpu.make_async_remote_copy(src_ref=src, dst_ref=dst, send_sem=sem_out, recv_sem=recv_sem,
                                          device_id=dev, device_id_type=MESH)
        return cp, to

    def to_side(src, dst, recv_sem, i):
        return message(src, dst, recv_sem, sides[1 - i], has_side[1 - i])

    def to_end(src, dst, recv_sem, j):
        return message(src, dst, recv_sem, ends[1 - j], has_end[1 - j])

    def to_diagonal(src, dst, recv_sem, i, j):
        return message(src, dst, recv_sem, diagonal[1 - i][1 - j], both(1 - i, 1 - j))

    def start(messages):
        for cp, to in messages:
            when(to, cp.start)

    def wait_units(sem, units):
        span = pool.at[pl.ds(0, 8 * units)]
        pltpu.make_async_copy(span, span, sem).wait()

    in_sides = has_side[0].astype(jnp.int32) + has_side[1].astype(jnp.int32)
    in_ends = has_end[0].astype(jnp.int32) + has_end[1].astype(jnp.int32)

    def wait_around(sem, units):
        for ns in (1, 2):
            for ne in (1, 2):

                @pl.when(jnp.logical_and(in_sides == ns, in_ends == ne))
                def _():
                    wait_units(sem, units(ns, ne))

    scl_units = scl_set.shape[1] // 16

    def halo_units(ns, ne):
        return ne * size + ns * ne * pairs + ns * 4 * size

    def all_units(ns, ne):
        fixed = 3 * 4 * species + 3 * scl_units
        around = scl_units * (ns + ne + ns * ne) + species * (6 * ns + ne)
        return fixed + around + count * halo_units(ns, ne)

    def part(k):
        return pl.ds(k * size, size)

    ahead = (ring[BLOCK - 1], ring[1])

    def far_messages(k):
        return [message(far.at[h, part(k)], via.at[h, part(k)], sem_far.at[k], ahead[h]) for h in range(2)]

    def near_messages(k):
        return [message(near.at[h, part(k)], got.at[1, h, part(k)], sem_regrid.at[k], ahead[1 - h]) for h in range(2)]

    def merged_messages(k):
        return [message(merged.at[h, part(k)], got.at[0, h, part(k)], sem_regrid.at[k], ahead[h]) for h in range(2)]

    def halo_messages(k):
        out = [to_end(edge.at[e, part(k)], got_edge.at[e, part(k)], sem_halo.at[k], e) for e in range(2)]
        out += [to_diagonal(tip.at[k, i, e], corner.at[k, i, e], sem_halo.at[k], i, e)
                for i in range(2) for e in range(2)]
        return out + [to_side(box.at[part(k)], beside.at[i, part(k)], sem_halo.at[k], i) for i in range(2)]

    scl_messages = [message(scl_cand.at[d - 1], scl_recv.at[BLOCK - d], sem_scl.at[0], ring[d]) for d in range(1, BLOCK)]
    scl_around = [to_side(scl_set.at[0], scl_beside.at[i, 0], sem_scl.at[1], i) for i in range(2)]
    scl_around += [to_end(scl_set.at[0], scl_set.at[1 + j], sem_scl.at[1], j) for j in range(2)]
    scl_around += [to_diagonal(scl_set.at[0], scl_beside.at[i, 1 + j], sem_scl.at[1], i, j)
                   for i in range(2) for j in range(2)]
    dif_ends = [to_end(dif_edge.at[e], dif_got.at[e], sem_dif.at[0], e) for e in range(2)]
    dif_sides = [to_side(dif, dif_beside.at[i], sem_dif.at[1], i) for i in range(2)]
    dif_corners = [to_side(dif_got, dif_corner.at[i], sem_dif.at[1], i) for i in range(2)]

    def each(n, act):
        def body(k, _):
            act(k)
            return 0

        lax.fori_loop(0, n, body, 0)

    own_load.wait()
    first_slot = [own_ref[0, 1, base + lax.rem(x + d, BLOCK)] == 0 for d in range(BLOCK)]
    holder = own_ref[0, 0, b]
    came = lax.rem(lax.rem(holder, BLOCK) + BLOCK - x, BLOCK)
    left, right = lax.rem(x + BLOCK - 1, BLOCK), lax.rem(x + 1, BLOCK)
    behind = (lax.rem(own_ref[0, 0, base + left], BLOCK) == right, lax.rem(own_ref[0, 0, base + right], BLOCK) == left)
    old_load.wait()

    def encode(s):
        codes, scales = [], []
        for t in range(2):
            layers = [old[t, s, a] for a in range(4)]
            m = jnp.maximum(jnp.maximum(jnp.abs(layers[0]), jnp.abs(layers[1])),
                            jnp.maximum(jnp.abs(layers[2]), jnp.abs(layers[3])))
            m = jnp.maximum(jnp.max(m, axis=0, keepdims=True), 1e-30)
            scale = (m * (1.004 / LEVELS)).astype(jnp.bfloat16).astype(jnp.float32)
            inv = 1.0 / scale
            rows = [jnp.round(v * inv).astype(jnp.int32) for v in layers]
            codes.append([jnp.concatenate(rows[2 * h:2 * h + 2], 0) for h in range(2)])
            scales.append(scale)

        def code(d, h):
            return jnp.where(first_slot[d], codes[0][h], codes[1][h]).astype(jnp.int16)

        for h in range(2):
            far[h, s] = code(2, h)
            near[h, s] = code((1, 3)[h], h)
            mine[h, s] = code((3, 1)[h], h)
            kept_own[h, s] = code(0, h)
        for d in range(BLOCK):
            scl_f32[d, pl.ds(s, 1)] = jnp.where(first_slot[d], scales[0], scales[1])

    each(species, encode)
    for d in range(1, BLOCK):
        scl_cand[d - 1] = scl_f32[d].astype(jnp.bfloat16)
    scl_recv[0] = scl_f32[0].astype(jnp.bfloat16)
    dif_load.wait()

    pl.semaphore_wait(barrier, BLOCK - 1 + in_sides + in_ends + in_sides * in_ends)

    each(count, lambda k: start(far_messages(k)))
    each(count, lambda k: start(near_messages(k)))
    start(scl_messages)
    start(dif_sides)

    def dif_pack(s):
        first, last = pack_edges([dif[s, a].astype(jnp.float32) for a in range(4)])
        dif_edge[0, s] = first.astype(jnp.bfloat16)
        dif_edge[1, s] = last.astype(jnp.bfloat16)

    each(species, dif_pack)
    start(dif_ends)

    def merge(k):
        wait_units(sem_far.at[k], 4 * size)
        for q in range(size):
            for h in range(2):
                s = k * size + q
                merged[h, s] = jnp.where(behind[h], via[h, s], mine[h, s])
        start(merged_messages(k))

    each(count, merge)

    wait_units(sem_scl.at[0], 3 * scl_units)
    scl_set[0] = scl_recv[came]
    start(scl_around)

    wait_around(sem_dif.at[0], lambda ns, ne: species * ne)
    start(dif_corners)

    def choose(k):
        wait_units(sem_regrid.at[k], 8 * size)
        for c in range(size):
            s = k * size + c
            layers = []
            for h in range(2):
                q = jnp.where(came == 0, kept_own[h, s], jnp.where(came == (3, 1)[h], got[1, h, s], got[0, h, s]))
                box[s, pl.ds(32 * h, 32)] = q
                q = q.astype(jnp.int32)
                layers += [q[0:16], q[16:32]]
            first, last = pack_edges(layers)
            edge[0, s] = first.astype(jnp.int16)
            edge[1, s] = last.astype(jnp.int16)
            tip_rows = pack_tips(first, last)
            for e in range(2):
                for i in range(2):
                    tips[i, e, c] = tip_rows[e][i]
        for i in range(2):
            for e in range(2):
                for m in range(tip.shape[3]):
                    pair = tips[i, e, pl.ds(2 * m, 2)].reshape(16, 128)
                    tip[k, i, e, m] = pair.astype(jnp.int16)
        start(halo_messages(k))

    each(count, choose)

    in_side = [there.astype(jnp.float32) for there in has_side]
    in_end = [there.astype(jnp.float32) for there in has_end]

    def kept(there, value):
        return jnp.where(there, value, 0.0)

    row = lax.broadcasted_iota(jnp.int32, (ZROWS, 128), 0)
    in_rows = jnp.where(row < 16, 1.0, jnp.where(row < 20, in_end[0], in_end[1]))

    wait_around(sem_dif.at[1], lambda ns, ne: 6 * species * ns)

    def weigh(at):
        for block, i in ((0, 0), (1, None), (2, 1)):
            for a in range(4):
                if i is None:
                    coef[4 * block + a, 0:16] = dif[at, a].astype(jnp.float32)
                else:
                    coef[4 * block + a, 0:16] = kept(has_side[i], dif_beside[i, at, a].astype(jnp.float32))
            tiles = [dif_got[j, at] if i is None else dif_corner[i, j, at] for j in range(2)]
            halo = unpack_edges(*[kept(both(i, j), tiles[j].astype(jnp.float32)) for j in range(2)])
            for a in range(4):
                coef[4 * block + a, 16:24] = halo[a]
        c = coef[0]
        from_layer = None
        for a in range(11):
            above = coef[a + 1]
            to_layer = 0.25 * (c + above)
            wts[at, a, 0] = to_layer
            if a:
                to_row = 0.25 * (c + pltpu.roll(c, ZROWS - 1, 0))
                to_column = 0.25 * (c + pltpu.roll(c, 127, 1))
                total = (to_layer + from_layer) + (to_row + pltpu.roll(to_row, 1, 0))
                total = total + (to_column + pltpu.roll(to_column, 1, 1))
                inverse = in_rows / (1.0 + total)
                if a < 4:
                    inverse = inverse * in_side[0]
                elif a > 7:
                    inverse = inverse * in_side[1]
                wts[at, a, 1] = to_row
                wts[at, a, 2] = to_column
                wts[at, a, 3] = inverse
            from_layer, c = to_layer, above

    each(species, weigh)

    wait_around(sem_scl.at[1], lambda ns, ne: scl_units * (ns + ne + ns * ne))
    for block, i in ((0, 0), (1, None), (2, 1)):
        rows = [(scl_set if i is None else scl_beside.at[i])[j].astype(jnp.float32) for j in range(3)]
        scl[block, 0] = rows[0] if i is None else kept(has_side[i], rows[0])
        for j in range(2):
            scl[block, 1 + j] = kept(both(i, j), rows[1 + j])

    def smooth(k):
        wait_around(sem_halo.at[k], halo_units)
        for i in range(2):
            for e in range(2):
                for m in range(tip.shape[3]):
                    pair = corner[k, i, e, m].astype(jnp.int32).astype(jnp.float32)
                    corner_f32[i, e, pl.ds(2 * m, 2)] = pair.reshape(2, 8, 128)
        for s in range(size):
            at = k * size + s
            for block, i in ((0, 0), (1, None), (2, 1)):
                scales = [scl[block, j, pl.ds(at, 1)] for j in range(3)]
                q = (box[at] if i is None else beside[i, at]).astype(jnp.int32).astype(jnp.float32) * scales[0]
                if i is None:
                    tiles = [got_edge[j, at].astype(jnp.int32).astype(jnp.float32) * scales[1 + j] for j in range(2)]
                    halo = dict(enumerate(unpack_edges(*tiles)))
                else:
                    halo = unpack_tips(i, *[corner_f32[i, j, s] * scales[1 + j] for j in range(2)])
                for a in range(4):
                    slab[s, 4 * block + a, 0:16] = q[16 * a:16 * a + 16]
                    if a in halo:
                        slab[s, 4 * block + a, 16:24] = halo[a]
        for it in range(ITERS):
            for s in range(size):
                at = k * size + s
                src = slab.at[s] if it == 0 else cur.at[(it - 1) % 2, s]
                below, v = src[it], src[it + 1]
                from_layer = wts[at, it, 0]
                for a in range(1 + it, 11 - it):
                    rows = 16 if it == ITERS - 1 or a in (1 + it, 10 - it) else ZROWS
                    above = src[a + 1]
                    to_layer, to_row, to_column, inverse = (wts[at, a, f] for f in range(4))
                    acc = slab[s, a] + from_layer * below + to_layer * above
                    acc = acc + (pltpu.roll(to_row * v, 1, 0) + to_row * pltpu.roll(v, ZROWS - 1, 0))
                    v_rows, to_rows = v[0:rows], to_column[0:rows]
                    acc = acc[0:rows] + (pltpu.roll(to_rows * v_rows, 1, 1) + to_rows * pltpu.roll(v_rows, 127, 1))
                    acc = acc * inverse[0:rows]
                    if it == ITERS - 1:
                        res[at, a - 4] = acc
                    else:
                        cur[it % 2, s, a, 0:rows] = acc
                    from_layer, below, v = to_layer, v, above

    each(count, smooth)
    wait_around(sem_out, all_units)


def local(old_state, owners, diffusivity):
    species = diffusivity.shape[0]
    size = 3 if species % 3 == 0 else 1
    count = species // size
    pairs, padded = (size + 1) // 2, (species + 15) // 16 * 16
    units = 18 * species + 3 * padded // 8 + padded + 14 * species + count * (10 * size + 4 * pairs)
    i16, i32, bf16, f32 = jnp.int16, jnp.int32, jnp.bfloat16, jnp.float32
    dma = pltpu.SemaphoreType.DMA
    halves = pltpu.VMEM((2, species, 32, 128), i16)
    scratch = [
        pltpu.SMEM(owners.shape, i32),
        pltpu.VMEM(old_state.shape, f32),
        halves, halves, halves, halves, halves,
        pltpu.VMEM((2, 2, species, 32, 128), i16),
        halves,
        pltpu.VMEM((species, 64, 128), i16),
        pltpu.VMEM((2, species, 64, 128), i16),
        pltpu.VMEM((2, species, 16, 128), i16),
        pltpu.VMEM((2, species, 16, 128), i16),
        pltpu.VMEM((2, 2, 2 * pairs, 8, 128), i32),
        pltpu.VMEM((count, 2, 2, pairs, 16, 128), i16),
        pltpu.VMEM((count, 2, 2, pairs, 16, 128), i16),
        pltpu.VMEM((2, 2, 2 * pairs, 8, 128), f32),
        pltpu.VMEM((4, padded, 128), f32),
        pltpu.VMEM((3, padded, 128), bf16),
        pltpu.VMEM((4, padded, 128), bf16),
        pltpu.VMEM((3, padded, 128), bf16),
        pltpu.VMEM((2, 3, padded, 128), bf16),
        pltpu.VMEM((3, 3, padded, 128), f32),
        pltpu.VMEM((species, 4, 16, 128), bf16),
        pltpu.VMEM((2, species, 16, 128), bf16),
        pltpu.VMEM((2, species, 4, 16, 128), bf16),
        pltpu.VMEM((2, species, 16, 128), bf16),
        pltpu.VMEM((2, 2, species, 16, 128), bf16),
        pltpu.VMEM((12, ZROWS, 128), f32),
        pltpu.VMEM((size, 12, ZROWS, 128), f32),
        pltpu.VMEM((2, size, 12, ZROWS, 128), f32),
        pltpu.VMEM((species, 11, 4, ZROWS, 128), f32),
        pltpu.VMEM((8 * units, 128), f32),
        dma((3,)), dma(()), dma((count,)), dma((count,)), dma((count,)), dma((2,)), dma((2,)),
    ]
    old_state, owners, diffusivity = (
        pltpu.with_memory_space_constraint(v, pltpu.HBM) for v in (old_state, owners, diffusivity)
    )
    return pl.pallas_call(
        kernel,
        out_shape=pltpu.VMEM(diffusivity.shape, f32),
        in_specs=[pl.BlockSpec(memory_space=pltpu.HBM)] * 3,
        out_specs=pl.BlockSpec(memory_space=pltpu.VMEM),
        scratch_shapes=scratch,
        name="regrid_smooth",
        compiler_params=pltpu.CompilerParams(collective_id=0, has_side_effects=True, vmem_limit_bytes=40 * 2**20),
    )(owners, old_state, diffusivity)


def solution(mesh):
    placed = (
        P(None, None, "group", "box", None),
        P("group", None, None),
        P(None, "group", "box", None),
    )
    return jax.shard_map(
        local, mesh=mesh, in_specs=placed, out_specs=P(None, "group", "box", None), check_vma=False
    )
```

```python
import jax
import jax.numpy as jnp
from jax import lax
from jax.experimental import pallas as pl
from jax.experimental.pallas import tpu as pltpu
from jax.sharding import PartitionSpec as P

MESH = pl.DeviceIdType.MESH
BLOCK = 4
ITERS = 4
LEVELS = 32767.0
ZROWS = 24


def when(condition, act):
    if condition is None:
        act()
    else:
        pl.when(condition)(act)


def low_rows():
    return lax.broadcasted_iota(jnp.int32, (8, 128), 0) < 4


def pack_edges(rows):
    low = low_rows()
    first, last = [], []
    for a in (0, 2):
        p, q = rows[a], rows[a + 1]
        first.append(jnp.where(low, p[0:8], pltpu.roll(q[0:8], 4, 0)))
        last.append(jnp.where(low, pltpu.roll(p[8:16], 4, 0), q[8:16]))
    return jnp.concatenate(first, 0), jnp.concatenate(last, 0)


def unpack_edges(after, before):
    low = low_rows()
    out = []
    for a in range(4):
        n = after[8 * (a // 2):8 * (a // 2) + 8]
        p = before[8 * (a // 2):8 * (a // 2) + 8]
        if a % 2 == 0:
            out.append(jnp.where(low, n, pltpu.roll(p, 4, 0)))
        else:
            out.append(jnp.where(low, pltpu.roll(n, 4, 0), p))
    return out


def pack_tips(first, last):
    row = lax.broadcasted_iota(jnp.int32, (8, 128), 0)
    f01, f23, l01, l23 = first[0:8], first[8:16], last[0:8], last[8:16]
    return (
        (jnp.where(row == 7, pltpu.roll(f01, 3, 0), f23), jnp.where(row == 3, pltpu.roll(f23, 3, 0), f01)),
        (jnp.where(row == 4, pltpu.roll(l01, 5, 0), l23), jnp.where(row == 0, pltpu.roll(l23, 5, 0), l01)),
    )


def unpack_tips(side, n, p):
    low = low_rows()
    if side == 0:
        return {
            3: jnp.where(low, pltpu.roll(n, 4, 0), p),
            2: jnp.where(low, n, pltpu.roll(p, 4, 0)),
            1: jnp.where(low, pltpu.roll(n, 1, 0), pltpu.roll(p, 3, 0)),
        }
    return {
        0: jnp.where(low, n, pltpu.roll(p, 4, 0)),
        1: jnp.where(low, pltpu.roll(n, 4, 0), p),
        2: jnp.where(low, pltpu.roll(n, 5, 0), pltpu.roll(p, 7, 0)),
    }


def kernel(own_hbm, old_ref, dif_ref, res, own_ref, old, far, via, near, mine, merged, got, kept_own, box, beside,
           edge, got_edge, tips, tip, corner, corner_f32, scl_f32, scl_cand, scl_recv, scl_set, scl_beside, scl,
           dif, dif_edge, dif_beside, dif_got, dif_corner, coef, slab, cur, wts, pool,
           sem_in, sem_out, sem_far, sem_regrid, sem_halo, sem_scl, sem_dif):
    species = dif_ref.shape[0]
    count, size, pairs = tip.shape[0], slab.shape[0], tip.shape[3]
    g, b = lax.axis_index("group"), lax.axis_index("box")
    groups, boxes = lax.axis_size("group"), lax.axis_size("box")
    x = lax.rem(b, BLOCK)
    base = b - x
    ring = [None] + [(g, base + lax.rem(x + d, BLOCK)) for d in range(1, BLOCK)]
    gs = (lax.rem(g + groups - 1, groups), lax.rem(g + 1, groups))
    bs = (lax.rem(b + 1, boxes), lax.rem(b + boxes - 1, boxes))
    sides = [(gs[0], b), (gs[1], b)]
    ends = [(g, bs[0]), (g, bs[1])]
    diagonal = [[(gs[i], bs[j]) for j in range(2)] for i in range(2)]
    has_side = [g > 0, g < groups - 1]
    has_end = [b < boxes - 1, b > 0]

    def both(i, j):
        return has_end[j] if i is None else jnp.logical_and(has_side[i], has_end[j])

    around = [(sides[i], has_side[i]) for i in range(2)] + [(ends[j], has_end[j]) for j in range(2)]
    around += [(diagonal[i][j], both(i, j)) for i in range(2) for j in range(2)]

    barrier = pltpu.get_barrier_semaphore()
    for dev in ring[1:]:
        pl.semaphore_signal(barrier, inc=1, device_id=dev, device_id_type=MESH)
    for dev, there in around:

        @pl.when(there)
        def _():
            pl.semaphore_signal(barrier, inc=1, device_id=dev, device_id_type=MESH)

    old_load = pltpu.make_async_copy(old_ref, old, sem_in.at[0])
    old_load.start()
    own_load = pltpu.make_async_copy(own_hbm, own_ref, sem_in.at[1])
    own_load.start()
    dif_load = pltpu.make_async_copy(dif_ref, dif, sem_in.at[2])
    dif_load.start()

    def message(src, dst, recv_sem, dev, to=None):
        cp = pltpu.make_async_remote_copy(src_ref=src, dst_ref=dst, send_sem=sem_out, recv_sem=recv_sem,
                                          device_id=dev, device_id_type=MESH)
        return cp, to

    def to_side(src, dst, recv_sem, i):
        return message(src, dst, recv_sem, sides[1 - i], has_side[1 - i])

    def to_end(src, dst, recv_sem, j):
        return message(src, dst, recv_sem, ends[1 - j], has_end[1 - j])

    def to_diagonal(src, dst, recv_sem, i, j):
        return message(src, dst, recv_sem, diagonal[1 - i][1 - j], both(1 - i, 1 - j))

    def start(messages):
        for cp, to in messages:
            when(to, cp.start)

    def wait_units(sem, units):
        span = pool.at[pl.ds(0, 8 * units)]
        pltpu.make_async_copy(span, span, sem).wait()

    in_sides = has_side[0].astype(jnp.int32) + has_side[1].astype(jnp.int32)
    in_ends = has_end[0].astype(jnp.int32) + has_end[1].astype(jnp.int32)

    def wait_around(sem, units):
        for ns in (1, 2):
            for ne in (1, 2):

                @pl.when(jnp.logical_and(in_sides == ns, in_ends == ne))
                def _():
                    wait_units(sem, units(ns, ne))

    scl_units = scl_set.shape[1] // 16

    def halo_units(ns, ne):
        return ne * size + ns * ne * pairs + ns * 4 * size

    def all_units(ns, ne):
        fixed = 3 * 4 * species + 3 * scl_units
        around = scl_units * (ns + ne + ns * ne) + species * (6 * ns + ne)
        return fixed + around + count * halo_units(ns, ne)

    def part(k):
        return pl.ds(k * size, size)

    ahead = (ring[BLOCK - 1], ring[1])

    def far_messages(k):
        return [message(far.at[h, part(k)], via.at[h, part(k)], sem_far.at[k], ahead[h]) for h in range(2)]

    def near_messages(k):
        return [message(near.at[h, part(k)], got.at[1, h, part(k)], sem_regrid.at[k], ahead[1 - h]) for h in range(2)]

    def merged_messages(k):
        return [message(merged.at[h, part(k)], got.at[0, h, part(k)], sem_regrid.at[k], ahead[h]) for h in range(2)]

    def halo_messages(k):
        out = [to_end(edge.at[e, part(k)], got_edge.at[e, part(k)], sem_halo.at[k], e) for e in range(2)]
        out += [to_diagonal(tip.at[k, i, e], corner.at[k, i, e], sem_halo.at[k], i, e)
                for i in range(2) for e in range(2)]
        return out + [to_side(box.at[part(k)], beside.at[i, part(k)], sem_halo.at[k], i) for i in range(2)]

    scl_messages = [message(scl_cand.at[d - 1], scl_recv.at[BLOCK - d], sem_scl.at[0], ring[d]) for d in range(1, BLOCK)]
    scl_around = [to_side(scl_set.at[0], scl_beside.at[i, 0], sem_scl.at[1], i) for i in range(2)]
    scl_around += [to_end(scl_set.at[0], scl_set.at[1 + j], sem_scl.at[1], j) for j in range(2)]
    scl_around += [to_diagonal(scl_set.at[0], scl_beside.at[i, 1 + j], sem_scl.at[1], i, j)
                   for i in range(2) for j in range(2)]
    dif_ends = [to_end(dif_edge.at[e], dif_got.at[e], sem_dif.at[0], e) for e in range(2)]
    dif_sides = [to_side(dif, dif_beside.at[i], sem_dif.at[1], i) for i in range(2)]
    dif_corners = [to_side(dif_got, dif_corner.at[i], sem_dif.at[1], i) for i in range(2)]

    def each(n, act):
        def body(k, _):
            act(k)
            return 0

        lax.fori_loop(0, n, body, 0)

    own_load.wait()
    first_slot = [own_ref[0, 1, base + lax.rem(x + d, BLOCK)] == 0 for d in range(BLOCK)]
    holder = own_ref[0, 0, b]
    came = lax.rem(lax.rem(holder, BLOCK) + BLOCK - x, BLOCK)
    left, right = lax.rem(x + BLOCK - 1, BLOCK), lax.rem(x + 1, BLOCK)
    behind = (lax.rem(own_ref[0, 0, base + left], BLOCK) == right, lax.rem(own_ref[0, 0, base + right], BLOCK) == left)
    old_load.wait()

    def encode(s):
        codes, scales = [], []
        for t in range(2):
            layers = [old[t, s, a] for a in range(4)]
            m = jnp.maximum(jnp.maximum(jnp.abs(layers[0]), jnp.abs(layers[1])),
                            jnp.maximum(jnp.abs(layers[2]), jnp.abs(layers[3])))
            m = jnp.maximum(jnp.max(m, axis=0, keepdims=True), 1e-30)
            scale = (m * (1.004 / LEVELS)).astype(jnp.bfloat16).astype(jnp.float32)
            inv = 1.0 / scale
            rows = [jnp.round(v * inv).astype(jnp.int32) for v in layers]
            codes.append([jnp.concatenate(rows[2 * h:2 * h + 2], 0) for h in range(2)])
            scales.append(scale)

        def code(d, h):
            return jnp.where(first_slot[d], codes[0][h], codes[1][h]).astype(jnp.int16)

        for h in range(2):
            far[h, s] = code(2, h)
            near[h, s] = code((1, 3)[h], h)
            mine[h, s] = code((3, 1)[h], h)
            kept_own[h, s] = code(0, h)
        for d in range(BLOCK):
            scl_f32[d, pl.ds(s, 1)] = jnp.where(first_slot[d], scales[0], scales[1])

    each(species, encode)
    for d in range(1, BLOCK):
        scl_cand[d - 1] = scl_f32[d].astype(jnp.bfloat16)
    scl_recv[0] = scl_f32[0].astype(jnp.bfloat16)
    dif_load.wait()

    pl.semaphore_wait(barrier, BLOCK - 1 + in_sides + in_ends + in_sides * in_ends)

    each(count, lambda k: start(far_messages(k)))
    each(count, lambda k: start(near_messages(k)))
    start(scl_messages)
    start(dif_sides)

    def dif_pack(s):
        first, last = pack_edges([dif[s, a].astype(jnp.float32) for a in range(4)])
        dif_edge[0, s] = first.astype(jnp.bfloat16)
        dif_edge[1, s] = last.astype(jnp.bfloat16)

    each(species, dif_pack)
    start(dif_ends)

    def merge(k):
        wait_units(sem_far.at[k], 4 * size)
        for q in range(size):
            for h in range(2):
                s = k * size + q
                merged[h, s] = jnp.where(behind[h], via[h, s], mine[h, s])
        start(merged_messages(k))

    each(count, merge)

    wait_units(sem_scl.at[0], 3 * scl_units)
    scl_set[0] = scl_recv[came]
    start(scl_around)

    wait_around(sem_dif.at[0], lambda ns, ne: species * ne)
    start(dif_corners)

    def choose(k):
        wait_units(sem_regrid.at[k], 8 * size)
        for c in range(size):
            s = k * size + c
            layers = []
            for h in range(2):
                q = jnp.where(came == 0, kept_own[h, s], jnp.where(came == (3, 1)[h], got[1, h, s], got[0, h, s]))
                box[s, pl.ds(32 * h, 32)] = q
                q = q.astype(jnp.int32)
                layers += [q[0:16], q[16:32]]
            first, last = pack_edges(layers)
            edge[0, s] = first.astype(jnp.int16)
            edge[1, s] = last.astype(jnp.int16)
            tip_rows = pack_tips(first, last)
            for e in range(2):
                for i in range(2):
                    tips[i, e, c] = tip_rows[e][i]
        for i in range(2):
            for e in range(2):
                for m in range(tip.shape[3]):
                    pair = tips[i, e, pl.ds(2 * m, 2)].reshape(16, 128)
                    tip[k, i, e, m] = pair.astype(jnp.int16)
        start(halo_messages(k))

    each(count, choose)

    in_side = [there.astype(jnp.float32) for there in has_side]
    in_end = [there.astype(jnp.float32) for there in has_end]

    def kept(there, value):
        return jnp.where(there, value, 0.0)

    row = lax.broadcasted_iota(jnp.int32, (ZROWS, 128), 0)
    in_rows = jnp.where(row < 16, 1.0, jnp.where(row < 20, in_end[0], in_end[1]))

    wait_around(sem_dif.at[1], lambda ns, ne: 6 * species * ns)

    def weigh(k):
        for s in range(size):
            at = k * size + s
            for block, i in ((0, 0), (1, None), (2, 1)):
                for a in range(4):
                    if i is None:
                        coef[s, 4 * block + a, 0:16] = dif[at, a].astype(jnp.float32)
                    else:
                        coef[s, 4 * block + a, 0:16] = kept(has_side[i], dif_beside[i, at, a].astype(jnp.float32))
                tiles = [dif_got[j, at] if i is None else dif_corner[i, j, at] for j in range(2)]
                halo = unpack_edges(*[kept(both(i, j), tiles[j].astype(jnp.float32)) for j in range(2)])
                for a in range(4):
                    coef[s, 4 * block + a, 16:24] = halo[a]
        for s in range(size):
            at = k * size + s
            c = coef[s, 0]
            from_layer = None
            for a in range(11):
                above = coef[s, a + 1]
                to_layer = 0.25 * (c + above)
                wts[at, a, 0] = to_layer
                if a:
                    to_row = 0.25 * (c + pltpu.roll(c, ZROWS - 1, 0))
                    to_column = 0.25 * (c + pltpu.roll(c, 127, 1))
                    total = (to_layer + from_layer) + (to_row + pltpu.roll(to_row, 1, 0))
                    total = total + (to_column + pltpu.roll(to_column, 1, 1))
                    inverse = in_rows / (1.0 + total)
                    if a < 4:
                        inverse = inverse * in_side[0]
                    elif a > 7:
                        inverse = inverse * in_side[1]
                    wts[at, a, 1] = to_row
                    wts[at, a, 2] = to_column
                    wts[at, a, 3] = inverse
                from_layer, c = to_layer, above

    each(count, weigh)

    wait_around(sem_scl.at[1], lambda ns, ne: scl_units * (ns + ne + ns * ne))
    for block, i in ((0, 0), (1, None), (2, 1)):
        rows = [(scl_set if i is None else scl_beside.at[i])[j].astype(jnp.float32) for j in range(3)]
        scl[block, 0] = rows[0] if i is None else kept(has_side[i], rows[0])
        for j in range(2):
            scl[block, 1 + j] = kept(both(i, j), rows[1 + j])

    def smooth(k):
        wait_around(sem_halo.at[k], halo_units)
        for i in range(2):
            for e in range(2):
                for m in range(tip.shape[3]):
                    pair = corner[k, i, e, m].astype(jnp.int32).astype(jnp.float32)
                    corner_f32[i, e, pl.ds(2 * m, 2)] = pair.reshape(2, 8, 128)
        for s in range(size):
            at = k * size + s
            for block, i in ((0, 0), (1, None), (2, 1)):
                scales = [scl[block, j, pl.ds(at, 1)] for j in range(3)]
                q = (box[at] if i is None else beside[i, at]).astype(jnp.int32).astype(jnp.float32) * scales[0]
                if i is None:
                    tiles = [got_edge[j, at].astype(jnp.int32).astype(jnp.float32) * scales[1 + j] for j in range(2)]
                    halo = dict(enumerate(unpack_edges(*tiles)))
                else:
                    halo = unpack_tips(i, *[corner_f32[i, j, s] * scales[1 + j] for j in range(2)])
                for a in range(4):
                    slab[s, 4 * block + a, 0:16] = q[16 * a:16 * a + 16]
                    if a in halo:
                        slab[s, 4 * block + a, 16:24] = halo[a]
        for it in range(ITERS):
            for s in range(size):
                at = k * size + s
                src = slab.at[s] if it == 0 else cur.at[(it - 1) % 2, s]
                below, v = src[it], src[it + 1]
                from_layer = wts[at, it, 0]
                for a in range(1 + it, 11 - it):
                    rows = 16 if it == ITERS - 1 or a in (1 + it, 10 - it) else ZROWS
                    above = src[a + 1]
                    to_layer, to_row, to_column, inverse = (wts[at, a, f] for f in range(4))
                    acc = slab[s, a] + from_layer * below + to_layer * above
                    acc = acc + (pltpu.roll(to_row * v, 1, 0) + to_row * pltpu.roll(v, ZROWS - 1, 0))
                    v_rows, to_rows = v[0:rows], to_column[0:rows]
                    acc = acc[0:rows] + (pltpu.roll(to_rows * v_rows, 1, 1) + to_rows * pltpu.roll(v_rows, 127, 1))
                    acc = acc * inverse[0:rows]
                    if it == ITERS - 1:
                        res[at, a - 4] = acc
                    else:
                        cur[it % 2, s, a, 0:rows] = acc
                    from_layer, below, v = to_layer, v, above

    each(count, smooth)
    wait_around(sem_out, all_units)


def local(old_state, owners, diffusivity):
    species = diffusivity.shape[0]
    size = 3 if species % 3 == 0 else 1
    count = species // size
    pairs, padded = (size + 1) // 2, (species + 15) // 16 * 16
    units = 18 * species + 3 * padded // 8 + padded + 14 * species + count * (10 * size + 4 * pairs)
    i16, i32, bf16, f32 = jnp.int16, jnp.int32, jnp.bfloat16, jnp.float32
    dma = pltpu.SemaphoreType.DMA
    halves = pltpu.VMEM((2, species, 32, 128), i16)
    scratch = [
        pltpu.SMEM(owners.shape, i32),
        pltpu.VMEM(old_state.shape, f32),
        halves, halves, halves, halves, halves,
        pltpu.VMEM((2, 2, species, 32, 128), i16),
        halves,
        pltpu.VMEM((species, 64, 128), i16),
        pltpu.VMEM((2, species, 64, 128), i16),
        pltpu.VMEM((2, species, 16, 128), i16),
        pltpu.VMEM((2, species, 16, 128), i16),
        pltpu.VMEM((2, 2, 2 * pairs, 8, 128), i32),
        pltpu.VMEM((count, 2, 2, pairs, 16, 128), i16),
        pltpu.VMEM((count, 2, 2, pairs, 16, 128), i16),
        pltpu.VMEM((2, 2, 2 * pairs, 8, 128), f32),
        pltpu.VMEM((4, padded, 128), f32),
        pltpu.VMEM((3, padded, 128), bf16),
        pltpu.VMEM((4, padded, 128), bf16),
        pltpu.VMEM((3, padded, 128), bf16),
        pltpu.VMEM((2, 3, padded, 128), bf16),
        pltpu.VMEM((3, 3, padded, 128), f32),
        pltpu.VMEM((species, 4, 16, 128), bf16),
        pltpu.VMEM((2, species, 16, 128), bf16),
        pltpu.VMEM((2, species, 4, 16, 128), bf16),
        pltpu.VMEM((2, species, 16, 128), bf16),
        pltpu.VMEM((2, 2, species, 16, 128), bf16),
        pltpu.VMEM((size, 12, ZROWS, 128), f32),
        pltpu.VMEM((size, 12, ZROWS, 128), f32),
        pltpu.VMEM((2, size, 12, ZROWS, 128), f32),
        pltpu.VMEM((species, 11, 4, ZROWS, 128), f32),
        pltpu.VMEM((8 * units, 128), f32),
        dma((3,)), dma(()), dma((count,)), dma((count,)), dma((count,)), dma((2,)), dma((2,)),
    ]
    old_state, owners, diffusivity = (
        pltpu.with_memory_space_constraint(v, pltpu.HBM) for v in (old_state, owners, diffusivity)
    )
    return pl.pallas_call(
        kernel,
        out_shape=pltpu.VMEM(diffusivity.shape, f32),
        in_specs=[pl.BlockSpec(memory_space=pltpu.HBM)] * 3,
        out_specs=pl.BlockSpec(memory_space=pltpu.VMEM),
        scratch_shapes=scratch,
        name="regrid_smooth",
        compiler_params=pltpu.CompilerParams(collective_id=0, has_side_effects=True, vmem_limit_bytes=40 * 2**20),
    )(owners, old_state, diffusivity)


def solution(mesh):
    placed = (
        P(None, None, "group", "box", None),
        P("group", None, None),
        P(None, "group", "box", None),
    )
    return jax.shard_map(
        local, mesh=mesh, in_specs=placed, out_specs=P(None, "group", "box", None), check_vma=False
    )
```

```python
import jax
import jax.numpy as jnp
from jax import lax
from jax.experimental import pallas as pl
from jax.experimental.pallas import tpu as pltpu
from jax.sharding import PartitionSpec as P

MESH = pl.DeviceIdType.MESH
BLOCK = 4
ITERS = 4
LEVELS = 32767.0
ZROWS = 24


def when(condition, act):
    if condition is None:
        act()
    else:
        pl.when(condition)(act)


def low_rows():
    return lax.broadcasted_iota(jnp.int32, (8, 128), 0) < 4


def pack_edges(rows):
    low = low_rows()
    first, last = [], []
    for a in (0, 2):
        p, q = rows[a], rows[a + 1]
        first.append(jnp.where(low, p[0:8], pltpu.roll(q[0:8], 4, 0)))
        last.append(jnp.where(low, pltpu.roll(p[8:16], 4, 0), q[8:16]))
    return jnp.concatenate(first, 0), jnp.concatenate(last, 0)


def unpack_edges(after, before):
    low = low_rows()
    out = []
    for a in range(4):
        n = after[8 * (a // 2):8 * (a // 2) + 8]
        p = before[8 * (a // 2):8 * (a // 2) + 8]
        if a % 2 == 0:
            out.append(jnp.where(low, n, pltpu.roll(p, 4, 0)))
        else:
            out.append(jnp.where(low, pltpu.roll(n, 4, 0), p))
    return out


def pack_tips(first, last):
    row = lax.broadcasted_iota(jnp.int32, (8, 128), 0)
    f01, f23, l01, l23 = first[0:8], first[8:16], last[0:8], last[8:16]
    return (
        (jnp.where(row == 7, pltpu.roll(f01, 3, 0), f23), jnp.where(row == 3, pltpu.roll(f23, 3, 0), f01)),
        (jnp.where(row == 4, pltpu.roll(l01, 5, 0), l23), jnp.where(row == 0, pltpu.roll(l23, 5, 0), l01)),
    )


def unpack_tips(side, n, p):
    low = low_rows()
    if side == 0:
        return {
            3: jnp.where(low, pltpu.roll(n, 4, 0), p),
            2: jnp.where(low, n, pltpu.roll(p, 4, 0)),
            1: jnp.where(low, pltpu.roll(n, 1, 0), pltpu.roll(p, 3, 0)),
        }
    return {
        0: jnp.where(low, n, pltpu.roll(p, 4, 0)),
        1: jnp.where(low, pltpu.roll(n, 4, 0), p),
        2: jnp.where(low, pltpu.roll(n, 5, 0), pltpu.roll(p, 7, 0)),
    }


def kernel(own_hbm, old_ref, dif_ref, res, own_ref, old, far, via, near, mine, merged, got, kept_own, box, beside,
           edge, got_edge, tips, tip, corner, corner_f32, scl_f32, scl_cand, scl_recv, scl_set, scl_beside, scl,
           dif, dif_edge, dif_beside, dif_got, dif_corner, coef, slab, cur, wts, pool,
           sem_in, sem_out, sem_far, sem_regrid, sem_halo, sem_scl, sem_dif):
    species = dif_ref.shape[0]
    count, size, pairs = tip.shape[0], slab.shape[0], tip.shape[3]
    g, b = lax.axis_index("group"), lax.axis_index("box")
    groups, boxes = lax.axis_size("group"), lax.axis_size("box")
    x = lax.rem(b, BLOCK)
    base = b - x
    ring = [None] + [(g, base + lax.rem(x + d, BLOCK)) for d in range(1, BLOCK)]
    gs = (lax.rem(g + groups - 1, groups), lax.rem(g + 1, groups))
    bs = (lax.rem(b + 1, boxes), lax.rem(b + boxes - 1, boxes))
    sides = [(gs[0], b), (gs[1], b)]
    ends = [(g, bs[0]), (g, bs[1])]
    diagonal = [[(gs[i], bs[j]) for j in range(2)] for i in range(2)]
    has_side = [g > 0, g < groups - 1]
    has_end = [b < boxes - 1, b > 0]

    def both(i, j):
        return has_end[j] if i is None else jnp.logical_and(has_side[i], has_end[j])

    around = [(sides[i], has_side[i]) for i in range(2)] + [(ends[j], has_end[j]) for j in range(2)]
    around += [(diagonal[i][j], both(i, j)) for i in range(2) for j in range(2)]

    barrier = pltpu.get_barrier_semaphore()
    for dev in ring[1:]:
        pl.semaphore_signal(barrier, inc=1, device_id=dev, device_id_type=MESH)
    for dev, there in around:

        @pl.when(there)
        def _():
            pl.semaphore_signal(barrier, inc=1, device_id=dev, device_id_type=MESH)

    old_load = pltpu.make_async_copy(old_ref, old, sem_in.at[0])
    old_load.start()
    own_load = pltpu.make_async_copy(own_hbm, own_ref, sem_in.at[1])
    own_load.start()
    dif_load = pltpu.make_async_copy(dif_ref, dif, sem_in.at[2])
    dif_load.start()

    def message(src, dst, recv_sem, dev, to=None):
        cp = pltpu.make_async_remote_copy(src_ref=src, dst_ref=dst, send_sem=sem_out, recv_sem=recv_sem,
                                          device_id=dev, device_id_type=MESH)
        return cp, to

    def to_side(src, dst, recv_sem, i):
        return message(src, dst, recv_sem, sides[1 - i], has_side[1 - i])

    def to_end(src, dst, recv_sem, j):
        return message(src, dst, recv_sem, ends[1 - j], has_end[1 - j])

    def to_diagonal(src, dst, recv_sem, i, j):
        return message(src, dst, recv_sem, diagonal[1 - i][1 - j], both(1 - i, 1 - j))

    def start(messages):
        for cp, to in messages:
            when(to, cp.start)

    def wait_units(sem, units):
        span = pool.at[pl.ds(0, 8 * units)]
        pltpu.make_async_copy(span, span, sem).wait()

    in_sides = has_side[0].astype(jnp.int32) + has_side[1].astype(jnp.int32)
    in_ends = has_end[0].astype(jnp.int32) + has_end[1].astype(jnp.int32)

    def wait_around(sem, units):
        for ns in (1, 2):
            for ne in (1, 2):

                @pl.when(jnp.logical_and(in_sides == ns, in_ends == ne))
                def _():
                    wait_units(sem, units(ns, ne))

    scl_units = scl_set.shape[1] // 16

    def halo_units(ns, ne):
        return ne * size + ns * ne * pairs + ns * 4 * size

    def all_units(ns, ne):
        fixed = 3 * 4 * species + 3 * scl_units
        around = scl_units * (ns + ne + ns * ne) + species * (6 * ns + ne)
        return fixed + around + count * halo_units(ns, ne)

    def part(k):
        return pl.ds(k * size, size)

    ahead = (ring[BLOCK - 1], ring[1])

    def far_messages(k):
        return [message(far.at[h, part(k)], via.at[h, part(k)], sem_far.at[k], ahead[h]) for h in range(2)]

    def near_messages(k):
        return [message(near.at[h, part(k)], got.at[1, h, part(k)], sem_regrid.at[k], ahead[1 - h]) for h in range(2)]

    def merged_messages(k):
        return [message(merged.at[h, part(k)], got.at[0, h, part(k)], sem_regrid.at[k], ahead[h]) for h in range(2)]

    def halo_messages(k):
        out = [to_end(edge.at[e, part(k)], got_edge.at[e, part(k)], sem_halo.at[k], e) for e in range(2)]
        out += [to_diagonal(tip.at[k, i, e], corner.at[k, i, e], sem_halo.at[k], i, e)
                for i in range(2) for e in range(2)]
        return out + [to_side(box.at[part(k)], beside.at[i, part(k)], sem_halo.at[k], i) for i in range(2)]

    scl_messages = [message(scl_cand.at[d - 1], scl_recv.at[BLOCK - d], sem_scl.at[0], ring[d]) for d in range(1, BLOCK)]
    scl_around = [to_side(scl_set.at[0], scl_beside.at[i, 0], sem_scl.at[1], i) for i in range(2)]
    scl_around += [to_end(scl_set.at[0], scl_set.at[1 + j], sem_scl.at[1], j) for j in range(2)]
    scl_around += [to_diagonal(scl_set.at[0], scl_beside.at[i, 1 + j], sem_scl.at[1], i, j)
                   for i in range(2) for j in range(2)]
    dif_ends = [to_end(dif_edge.at[e], dif_got.at[e], sem_dif.at[0], e) for e in range(2)]
    dif_sides = [to_side(dif, dif_beside.at[i], sem_dif.at[1], i) for i in range(2)]
    dif_corners = [to_side(dif_got, dif_corner.at[i], sem_dif.at[1], i) for i in range(2)]

    def each(n, act):
        def body(k, _):
            act(k)
            return 0

        lax.fori_loop(0, n, body, 0)

    own_load.wait()
    first_slot = [own_ref[0, 1, base + lax.rem(x + d, BLOCK)] == 0 for d in range(BLOCK)]
    holder = own_ref[0, 0, b]
    came = lax.rem(lax.rem(holder, BLOCK) + BLOCK - x, BLOCK)
    left, right = lax.rem(x + BLOCK - 1, BLOCK), lax.rem(x + 1, BLOCK)
    behind = (lax.rem(own_ref[0, 0, base + left], BLOCK) == right, lax.rem(own_ref[0, 0, base + right], BLOCK) == left)
    old_load.wait()

    def encode(s):
        codes, scales = [], []
        for t in range(2):
            layers = [old[t, s, a] for a in range(4)]
            m = jnp.maximum(jnp.maximum(jnp.abs(layers[0]), jnp.abs(layers[1])),
                            jnp.maximum(jnp.abs(layers[2]), jnp.abs(layers[3])))
            m = jnp.maximum(jnp.max(m, axis=0, keepdims=True), 1e-30)
            scale = (m * (1.004 / LEVELS)).astype(jnp.bfloat16).astype(jnp.float32)
            inv = 1.0 / scale
            rows = [jnp.round(v * inv).astype(jnp.int32) for v in layers]
            codes.append([jnp.concatenate(rows[2 * h:2 * h + 2], 0) for h in range(2)])
            scales.append(scale)

        def code(d, h):
            return jnp.where(first_slot[d], codes[0][h], codes[1][h]).astype(jnp.int16)

        for h in range(2):
            far[h, s] = code(2, h)
            near[h, s] = code((1, 3)[h], h)
            mine[h, s] = code((3, 1)[h], h)
            kept_own[h, s] = code(0, h)
        for d in range(BLOCK):
            scl_f32[d, pl.ds(s, 1)] = jnp.where(first_slot[d], scales[0], scales[1])

    each(species, encode)
    for d in range(1, BLOCK):
        scl_cand[d - 1] = scl_f32[d].astype(jnp.bfloat16)
    scl_recv[0] = scl_f32[0].astype(jnp.bfloat16)
    dif_load.wait()

    pl.semaphore_wait(barrier, BLOCK - 1 + in_sides + in_ends + in_sides * in_ends)

    each(count, lambda k: start(far_messages(k)))
    start(dif_sides)

    def dif_pack(s):
        first, last = pack_edges([dif[s, a].astype(jnp.float32) for a in range(4)])
        dif_edge[0, s] = first.astype(jnp.bfloat16)
        dif_edge[1, s] = last.astype(jnp.bfloat16)

    each(species, dif_pack)
    start(dif_ends)
    each(count, lambda k: start(near_messages(k)))
    start(scl_messages)

    def merge(k):
        wait_units(sem_far.at[k], 4 * size)
        for q in range(size):
            for h in range(2):
                s = k * size + q
                merged[h, s] = jnp.where(behind[h], via[h, s], mine[h, s])
        start(merged_messages(k))

    each(count, merge)

    wait_units(sem_scl.at[0], 3 * scl_units)
    scl_set[0] = scl_recv[came]
    start(scl_around)

    wait_around(sem_dif.at[0], lambda ns, ne: species * ne)
    start(dif_corners)

    def choose(k):
        wait_units(sem_regrid.at[k], 8 * size)
        for c in range(size):
            s = k * size + c
            layers = []
            for h in range(2):
                q = jnp.where(came == 0, kept_own[h, s], jnp.where(came == (3, 1)[h], got[1, h, s], got[0, h, s]))
                box[s, pl.ds(32 * h, 32)] = q
                q = q.astype(jnp.int32)
                layers += [q[0:16], q[16:32]]
            first, last = pack_edges(layers)
            edge[0, s] = first.astype(jnp.int16)
            edge[1, s] = last.astype(jnp.int16)
            tip_rows = pack_tips(first, last)
            for e in range(2):
                for i in range(2):
                    tips[i, e, c] = tip_rows[e][i]
        for i in range(2):
            for e in range(2):
                for m in range(tip.shape[3]):
                    pair = tips[i, e, pl.ds(2 * m, 2)].reshape(16, 128)
                    tip[k, i, e, m] = pair.astype(jnp.int16)
        start(halo_messages(k))

    each(count, choose)

    in_side = [there.astype(jnp.float32) for there in has_side]
    in_end = [there.astype(jnp.float32) for there in has_end]

    def kept(there, value):
        return jnp.where(there, value, 0.0)

    row = lax.broadcasted_iota(jnp.int32, (ZROWS, 128), 0)
    in_rows = jnp.where(row < 16, 1.0, jnp.where(row < 20, in_end[0], in_end[1]))

    wait_around(sem_dif.at[1], lambda ns, ne: 6 * species * ns)

    def weigh(k):
        for s in range(size):
            at = k * size + s
            for block, i in ((0, 0), (1, None), (2, 1)):
                for a in range(4):
                    if i is None:
                        coef[s, 4 * block + a, 0:16] = dif[at, a].astype(jnp.float32)
                    else:
                        coef[s, 4 * block + a, 0:16] = kept(has_side[i], dif_beside[i, at, a].astype(jnp.float32))
                tiles = [dif_got[j, at] if i is None else dif_corner[i, j, at] for j in range(2)]
                halo = unpack_edges(*[kept(both(i, j), tiles[j].astype(jnp.float32)) for j in range(2)])
                for a in range(4):
                    coef[s, 4 * block + a, 16:24] = halo[a]
        for s in range(size):
            at = k * size + s
            c = coef[s, 0]
            from_layer = None
            for a in range(11):
                above = coef[s, a + 1]
                to_layer = 0.25 * (c + above)
                wts[at, a, 0] = to_layer
                if a:
                    to_row = 0.25 * (c + pltpu.roll(c, ZROWS - 1, 0))
                    to_column = 0.25 * (c + pltpu.roll(c, 127, 1))
                    total = (to_layer + from_layer) + (to_row + pltpu.roll(to_row, 1, 0))
                    total = total + (to_column + pltpu.roll(to_column, 1, 1))
                    inverse = in_rows / (1.0 + total)
                    if a < 4:
                        inverse = inverse * in_side[0]
                    elif a > 7:
                        inverse = inverse * in_side[1]
                    wts[at, a, 1] = to_row
                    wts[at, a, 2] = to_column
                    wts[at, a, 3] = inverse
                from_layer, c = to_layer, above

    each(count, weigh)

    wait_around(sem_scl.at[1], lambda ns, ne: scl_units * (ns + ne + ns * ne))
    for block, i in ((0, 0), (1, None), (2, 1)):
        rows = [(scl_set if i is None else scl_beside.at[i])[j].astype(jnp.float32) for j in range(3)]
        scl[block, 0] = rows[0] if i is None else kept(has_side[i], rows[0])
        for j in range(2):
            scl[block, 1 + j] = kept(both(i, j), rows[1 + j])

    def smooth(k):
        wait_around(sem_halo.at[k], halo_units)
        for i in range(2):
            for e in range(2):
                for m in range(tip.shape[3]):
                    pair = corner[k, i, e, m].astype(jnp.int32).astype(jnp.float32)
                    corner_f32[i, e, pl.ds(2 * m, 2)] = pair.reshape(2, 8, 128)
        for s in range(size):
            at = k * size + s
            for block, i in ((0, 0), (1, None), (2, 1)):
                scales = [scl[block, j, pl.ds(at, 1)] for j in range(3)]
                q = (box[at] if i is None else beside[i, at]).astype(jnp.int32).astype(jnp.float32) * scales[0]
                if i is None:
                    tiles = [got_edge[j, at].astype(jnp.int32).astype(jnp.float32) * scales[1 + j] for j in range(2)]
                    halo = dict(enumerate(unpack_edges(*tiles)))
                else:
                    halo = unpack_tips(i, *[corner_f32[i, j, s] * scales[1 + j] for j in range(2)])
                for a in range(4):
                    slab[s, 4 * block + a, 0:16] = q[16 * a:16 * a + 16]
                    if a in halo:
                        slab[s, 4 * block + a, 16:24] = halo[a]
        for it in range(ITERS):
            for s in range(size):
                at = k * size + s
                src = slab.at[s] if it == 0 else cur.at[(it - 1) % 2, s]
                below, v = src[it], src[it + 1]
                from_layer = wts[at, it, 0]
                for a in range(1 + it, 11 - it):
                    rows = 16 if it == ITERS - 1 or a in (1 + it, 10 - it) else ZROWS
                    above = src[a + 1]
                    to_layer, to_row, to_column, inverse = (wts[at, a, f] for f in range(4))
                    acc = slab[s, a] + from_layer * below + to_layer * above
                    acc = acc + (pltpu.roll(to_row * v, 1, 0) + to_row * pltpu.roll(v, ZROWS - 1, 0))
                    v_rows, to_rows = v[0:rows], to_column[0:rows]
                    acc = acc[0:rows] + (pltpu.roll(to_rows * v_rows, 1, 1) + to_rows * pltpu.roll(v_rows, 127, 1))
                    acc = acc * inverse[0:rows]
                    if it == ITERS - 1:
                        res[at, a - 4] = acc
                    else:
                        cur[it % 2, s, a, 0:rows] = acc
                    from_layer, below, v = to_layer, v, above

    each(count, smooth)
    wait_around(sem_out, all_units)


def local(old_state, owners, diffusivity):
    species = diffusivity.shape[0]
    size = 3 if species % 3 == 0 else 1
    count = species // size
    pairs, padded = (size + 1) // 2, (species + 15) // 16 * 16
    units = 18 * species + 3 * padded // 8 + padded + 14 * species + count * (10 * size + 4 * pairs)
    i16, i32, bf16, f32 = jnp.int16, jnp.int32, jnp.bfloat16, jnp.float32
    dma = pltpu.SemaphoreType.DMA
    halves = pltpu.VMEM((2, species, 32, 128), i16)
    scratch = [
        pltpu.SMEM(owners.shape, i32),
        pltpu.VMEM(old_state.shape, f32),
        halves, halves, halves, halves, halves,
        pltpu.VMEM((2, 2, species, 32, 128), i16),
        halves,
        pltpu.VMEM((species, 64, 128), i16),
        pltpu.VMEM((2, species, 64, 128), i16),
        pltpu.VMEM((2, species, 16, 128), i16),
        pltpu.VMEM((2, species, 16, 128), i16),
        pltpu.VMEM((2, 2, 2 * pairs, 8, 128), i32),
        pltpu.VMEM((count, 2, 2, pairs, 16, 128), i16),
        pltpu.VMEM((count, 2, 2, pairs, 16, 128), i16),
        pltpu.VMEM((2, 2, 2 * pairs, 8, 128), f32),
        pltpu.VMEM((4, padded, 128), f32),
        pltpu.VMEM((3, padded, 128), bf16),
        pltpu.VMEM((4, padded, 128), bf16),
        pltpu.VMEM((3, padded, 128), bf16),
        pltpu.VMEM((2, 3, padded, 128), bf16),
        pltpu.VMEM((3, 3, padded, 128), f32),
        pltpu.VMEM((species, 4, 16, 128), bf16),
        pltpu.VMEM((2, species, 16, 128), bf16),
        pltpu.VMEM((2, species, 4, 16, 128), bf16),
        pltpu.VMEM((2, species, 16, 128), bf16),
        pltpu.VMEM((2, 2, species, 16, 128), bf16),
        pltpu.VMEM((size, 12, ZROWS, 128), f32),
        pltpu.VMEM((size, 12, ZROWS, 128), f32),
        pltpu.VMEM((2, size, 12, ZROWS, 128), f32),
        pltpu.VMEM((species, 11, 4, ZROWS, 128), f32),
        pltpu.VMEM((8 * units, 128), f32),
        dma((3,)), dma(()), dma((count,)), dma((count,)), dma((count,)), dma((2,)), dma((2,)),
    ]
    old_state, owners, diffusivity = (
        pltpu.with_memory_space_constraint(v, pltpu.HBM) for v in (old_state, owners, diffusivity)
    )
    return pl.pallas_call(
        kernel,
        out_shape=pltpu.VMEM(diffusivity.shape, f32),
        in_specs=[pl.BlockSpec(memory_space=pltpu.HBM)] * 3,
        out_specs=pl.BlockSpec(memory_space=pltpu.VMEM),
        scratch_shapes=scratch,
        name="regrid_smooth",
        compiler_params=pltpu.CompilerParams(collective_id=0, has_side_effects=True, vmem_limit_bytes=40 * 2**20),
    )(owners, old_state, diffusivity)


def solution(mesh):
    placed = (
        P(None, None, "group", "box", None),
        P("group", None, None),
        P(None, "group", "box", None),
    )
    return jax.shard_map(
        local, mesh=mesh, in_specs=placed, out_specs=P(None, "group", "box", None), check_vma=False
    )
```

```python
import jax
import jax.numpy as jnp
from jax import lax
from jax.experimental import pallas as pl
from jax.experimental.pallas import tpu as pltpu
from jax.sharding import PartitionSpec as P

MESH = pl.DeviceIdType.MESH
BLOCK = 4
ITERS = 4
LEVELS = 32767.0
ZROWS = 24


def when(condition, act):
    if condition is None:
        act()
    else:
        pl.when(condition)(act)


def low_rows():
    return lax.broadcasted_iota(jnp.int32, (8, 128), 0) < 4


def pack_edges(rows):
    low = low_rows()
    first, last = [], []
    for a in (0, 2):
        p, q = rows[a], rows[a + 1]
        first.append(jnp.where(low, p[0:8], pltpu.roll(q[0:8], 4, 0)))
        last.append(jnp.where(low, pltpu.roll(p[8:16], 4, 0), q[8:16]))
    return jnp.concatenate(first, 0), jnp.concatenate(last, 0)


def unpack_edges(after, before):
    low = low_rows()
    out = []
    for a in range(4):
        n = after[8 * (a // 2):8 * (a // 2) + 8]
        p = before[8 * (a // 2):8 * (a // 2) + 8]
        if a % 2 == 0:
            out.append(jnp.where(low, n, pltpu.roll(p, 4, 0)))
        else:
            out.append(jnp.where(low, pltpu.roll(n, 4, 0), p))
    return out


def pack_tips(first, last):
    row = lax.broadcasted_iota(jnp.int32, (8, 128), 0)
    f01, f23, l01, l23 = first[0:8], first[8:16], last[0:8], last[8:16]
    return (
        (jnp.where(row == 7, pltpu.roll(f01, 3, 0), f23), jnp.where(row == 3, pltpu.roll(f23, 3, 0), f01)),
        (jnp.where(row == 4, pltpu.roll(l01, 5, 0), l23), jnp.where(row == 0, pltpu.roll(l23, 5, 0), l01)),
    )


def unpack_tips(side, n, p):
    low = low_rows()
    if side == 0:
        return {
            3: jnp.where(low, pltpu.roll(n, 4, 0), p),
            2: jnp.where(low, n, pltpu.roll(p, 4, 0)),
            1: jnp.where(low, pltpu.roll(n, 1, 0), pltpu.roll(p, 3, 0)),
        }
    return {
        0: jnp.where(low, n, pltpu.roll(p, 4, 0)),
        1: jnp.where(low, pltpu.roll(n, 4, 0), p),
        2: jnp.where(low, pltpu.roll(n, 5, 0), pltpu.roll(p, 7, 0)),
    }


def kernel(own_hbm, old_ref, dif_ref, res, own_ref, old, far, via, near, mine, merged, got, kept_own, box, beside,
           edge, got_edge, tips, tip, corner, corner_f32, scl_f32, scl_cand, scl_recv, scl_set, scl_beside, scl,
           dif, dif_edge, dif_beside, dif_got, dif_corner, coef, slab, cur, wts, pool,
           sem_in, sem_out, sem_far, sem_regrid, sem_halo, sem_scl, sem_dif):
    species = dif_ref.shape[0]
    count, size, pairs = tip.shape[0], slab.shape[0], tip.shape[3]
    g, b = lax.axis_index("group"), lax.axis_index("box")
    groups, boxes = lax.axis_size("group"), lax.axis_size("box")
    x = lax.rem(b, BLOCK)
    base = b - x
    ring = [None] + [(g, base + lax.rem(x + d, BLOCK)) for d in range(1, BLOCK)]
    gs = (lax.rem(g + groups - 1, groups), lax.rem(g + 1, groups))
    bs = (lax.rem(b + 1, boxes), lax.rem(b + boxes - 1, boxes))
    sides = [(gs[0], b), (gs[1], b)]
    ends = [(g, bs[0]), (g, bs[1])]
    diagonal = [[(gs[i], bs[j]) for j in range(2)] for i in range(2)]
    has_side = [g > 0, g < groups - 1]
    has_end = [b < boxes - 1, b > 0]

    def both(i, j):
        return has_end[j] if i is None else jnp.logical_and(has_side[i], has_end[j])

    around = [(sides[i], has_side[i]) for i in range(2)] + [(ends[j], has_end[j]) for j in range(2)]
    around += [(diagonal[i][j], both(i, j)) for i in range(2) for j in range(2)]

    barrier = pltpu.get_barrier_semaphore()
    for dev in ring[1:]:
        pl.semaphore_signal(barrier, inc=1, device_id=dev, device_id_type=MESH)
    for dev, there in around:

        @pl.when(there)
        def _():
            pl.semaphore_signal(barrier, inc=1, device_id=dev, device_id_type=MESH)

    old_load = pltpu.make_async_copy(old_ref, old, sem_in.at[0])
    old_load.start()
    own_load = pltpu.make_async_copy(own_hbm, own_ref, sem_in.at[1])
    own_load.start()
    dif_load = pltpu.make_async_copy(dif_ref, dif, sem_in.at[2])
    dif_load.start()

    def message(src, dst, recv_sem, dev, to=None):
        cp = pltpu.make_async_remote_copy(src_ref=src, dst_ref=dst, send_sem=sem_out, recv_sem=recv_sem,
                                          device_id=dev, device_id_type=MESH)
        return cp, to

    def to_side(src, dst, recv_sem, i):
        return message(src, dst, recv_sem, sides[1 - i], has_side[1 - i])

    def to_end(src, dst, recv_sem, j):
        return message(src, dst, recv_sem, ends[1 - j], has_end[1 - j])

    def to_diagonal(src, dst, recv_sem, i, j):
        return message(src, dst, recv_sem, diagonal[1 - i][1 - j], both(1 - i, 1 - j))

    def start(messages):
        for cp, to in messages:
            when(to, cp.start)

    def wait_units(sem, units):
        span = pool.at[pl.ds(0, 8 * units)]
        pltpu.make_async_copy(span, span, sem).wait()

    in_sides = has_side[0].astype(jnp.int32) + has_side[1].astype(jnp.int32)
    in_ends = has_end[0].astype(jnp.int32) + has_end[1].astype(jnp.int32)

    def wait_around(sem, units):
        for ns in (1, 2):
            for ne in (1, 2):

                @pl.when(jnp.logical_and(in_sides == ns, in_ends == ne))
                def _():
                    wait_units(sem, units(ns, ne))

    scl_units = scl_set.shape[1] // 16

    def halo_units(ns, ne):
        return ne * size + ns * ne * pairs + ns * 4 * size

    def all_units(ns, ne):
        fixed = 3 * 4 * species + 3 * scl_units
        around = scl_units * (ns + ne + ns * ne) + species * (6 * ns + ne)
        return fixed + around + count * halo_units(ns, ne)

    def part(k):
        return pl.ds(k * size, size)

    ahead = (ring[BLOCK - 1], ring[1])

    def far_messages(k):
        return [message(far.at[h, part(k)], via.at[h, part(k)], sem_far.at[k], ahead[h]) for h in range(2)]

    def near_messages(k):
        return [message(near.at[h, part(k)], got.at[1, h, part(k)], sem_regrid.at[k], ahead[1 - h]) for h in range(2)]

    def merged_messages(k):
        return [message(merged.at[h, part(k)], got.at[0, h, part(k)], sem_regrid.at[k], ahead[h]) for h in range(2)]

    def halo_messages(k):
        out = [to_side(box.at[part(k)], beside.at[i, part(k)], sem_halo.at[k], i) for i in range(2)]
        out += [to_end(edge.at[e, part(k)], got_edge.at[e, part(k)], sem_halo.at[k], e) for e in range(2)]
        return out + [to_diagonal(tip.at[k, i, e], corner.at[k, i, e], sem_halo.at[k], i, e)
                      for i in range(2) for e in range(2)]

    scl_messages = [message(scl_cand.at[d - 1], scl_recv.at[BLOCK - d], sem_scl.at[0], ring[d]) for d in range(1, BLOCK)]
    scl_around = [to_side(scl_set.at[0], scl_beside.at[i, 0], sem_scl.at[1], i) for i in range(2)]
    scl_around += [to_end(scl_set.at[0], scl_set.at[1 + j], sem_scl.at[1], j) for j in range(2)]
    scl_around += [to_diagonal(scl_set.at[0], scl_beside.at[i, 1 + j], sem_scl.at[1], i, j)
                   for i in range(2) for j in range(2)]
    dif_ends = [to_end(dif_edge.at[e], dif_got.at[e], sem_dif.at[0], e) for e in range(2)]
    dif_sides = [to_side(dif, dif_beside.at[i], sem_dif.at[1], i) for i in range(2)]
    dif_corners = [to_side(dif_got, dif_corner.at[i], sem_dif.at[1], i) for i in range(2)]

    def each(n, act):
        def body(k, _):
            act(k)
            return 0

        lax.fori_loop(0, n, body, 0)

    own_load.wait()
    first_slot = [own_ref[0, 1, base + lax.rem(x + d, BLOCK)] == 0 for d in range(BLOCK)]
    holder = own_ref[0, 0, b]
    came = lax.rem(lax.rem(holder, BLOCK) + BLOCK - x, BLOCK)
    left, right = lax.rem(x + BLOCK - 1, BLOCK), lax.rem(x + 1, BLOCK)
    behind = (lax.rem(own_ref[0, 0, base + left], BLOCK) == right, lax.rem(own_ref[0, 0, base + right], BLOCK) == left)
    old_load.wait()

    def encode(s):
        codes, scales = [], []
        for t in range(2):
            layers = [old[t, s, a] for a in range(4)]
            m = jnp.maximum(jnp.maximum(jnp.abs(layers[0]), jnp.abs(layers[1])),
                            jnp.maximum(jnp.abs(layers[2]), jnp.abs(layers[3])))
            m = jnp.maximum(jnp.max(m, axis=0, keepdims=True), 1e-30)
            scale = (m * (1.004 / LEVELS)).astype(jnp.bfloat16).astype(jnp.float32)
            inv = 1.0 / scale
            rows = [jnp.round(v * inv).astype(jnp.int32) for v in layers]
            codes.append([jnp.concatenate(rows[2 * h:2 * h + 2], 0) for h in range(2)])
            scales.append(scale)

        def code(d, h):
            return jnp.where(first_slot[d], codes[0][h], codes[1][h]).astype(jnp.int16)

        for h in range(2):
            far[h, s] = code(2, h)
            near[h, s] = code((1, 3)[h], h)
            mine[h, s] = code((3, 1)[h], h)
            kept_own[h, s] = code(0, h)
        for d in range(BLOCK):
            scl_f32[d, pl.ds(s, 1)] = jnp.where(first_slot[d], scales[0], scales[1])

    each(species, encode)
    for d in range(1, BLOCK):
        scl_cand[d - 1] = scl_f32[d].astype(jnp.bfloat16)
    scl_recv[0] = scl_f32[0].astype(jnp.bfloat16)
    dif_load.wait()

    pl.semaphore_wait(barrier, BLOCK - 1 + in_sides + in_ends + in_sides * in_ends)

    each(count, lambda k: start(far_messages(k)))
    each(count, lambda k: start(near_messages(k)))
    start(scl_messages)
    start(dif_sides)

    def dif_pack(s):
        first, last = pack_edges([dif[s, a].astype(jnp.float32) for a in range(4)])
        dif_edge[0, s] = first.astype(jnp.bfloat16)
        dif_edge[1, s] = last.astype(jnp.bfloat16)

    each(species, dif_pack)
    start(dif_ends)

    def merge(k):
        wait_units(sem_far.at[k], 4 * size)
        for q in range(size):
            for h in range(2):
                s = k * size + q
                merged[h, s] = jnp.where(behind[h], via[h, s], mine[h, s])
        start(merged_messages(k))

    each(count, merge)

    wait_units(sem_scl.at[0], 3 * scl_units)
    scl_set[0] = scl_recv[came]
    start(scl_around)

    wait_around(sem_dif.at[0], lambda ns, ne: species * ne)
    start(dif_corners)

    def choose(k):
        wait_units(sem_regrid.at[k], 8 * size)
        for c in range(size):
            s = k * size + c
            layers = []
            for h in range(2):
                q = jnp.where(came == 0, kept_own[h, s], jnp.where(came == (3, 1)[h], got[1, h, s], got[0, h, s]))
                box[s, pl.ds(32 * h, 32)] = q
                q = q.astype(jnp.int32)
                layers += [q[0:16], q[16:32]]
            first, last = pack_edges(layers)
            edge[0, s] = first.astype(jnp.int16)
            edge[1, s] = last.astype(jnp.int16)
            tip_rows = pack_tips(first, last)
            for e in range(2):
                for i in range(2):
                    tips[i, e, c] = tip_rows[e][i]
        for i in range(2):
            for e in range(2):
                for m in range(tip.shape[3]):
                    pair = tips[i, e, pl.ds(2 * m, 2)].reshape(16, 128)
                    tip[k, i, e, m] = pair.astype(jnp.int16)
        start(halo_messages(k))

    each(count, choose)

    in_side = [there.astype(jnp.float32) for there in has_side]
    in_end = [there.astype(jnp.float32) for there in has_end]

    def kept(there, value):
        return jnp.where(there, value, 0.0)

    row = lax.broadcasted_iota(jnp.int32, (ZROWS, 128), 0)
    in_rows = jnp.where(row < 16, 1.0, jnp.where(row < 20, in_end[0], in_end[1]))

    wait_around(sem_dif.at[1], lambda ns, ne: 6 * species * ns)

    def weigh(k):
        for s in range(size):
            at = k * size + s
            for block, i in ((0, 0), (1, None), (2, 1)):
                for a in range(4):
                    if i is None:
                        coef[s, 4 * block + a, 0:16] = dif[at, a].astype(jnp.float32)
                    else:
                        coef[s, 4 * block + a, 0:16] = kept(has_side[i], dif_beside[i, at, a].astype(jnp.float32))
                tiles = [dif_got[j, at] if i is None else dif_corner[i, j, at] for j in range(2)]
                halo = unpack_edges(*[kept(both(i, j), tiles[j].astype(jnp.float32)) for j in range(2)])
                for a in range(4):
                    coef[s, 4 * block + a, 16:24] = halo[a]
        for s in range(size):
            at = k * size + s
            c = coef[s, 0]
            from_layer = None
            for a in range(11):
                above = coef[s, a + 1]
                to_layer = 0.25 * (c + above)
                wts[at, a, 0] = to_layer
                if a:
                    to_row = 0.25 * (c + pltpu.roll(c, ZROWS - 1, 0))
                    to_column = 0.25 * (c + pltpu.roll(c, 127, 1))
                    total = (to_layer + from_layer) + (to_row + pltpu.roll(to_row, 1, 0))
                    total = total + (to_column + pltpu.roll(to_column, 1, 1))
                    inverse = in_rows / (1.0 + total)
                    if a < 4:
                        inverse = inverse * in_side[0]
                    elif a > 7:
                        inverse = inverse * in_side[1]
                    wts[at, a, 1] = to_row
                    wts[at, a, 2] = to_column
                    wts[at, a, 3] = inverse
                from_layer, c = to_layer, above

    each(count, weigh)

    wait_around(sem_scl.at[1], lambda ns, ne: scl_units * (ns + ne + ns * ne))
    for block, i in ((0, 0), (1, None), (2, 1)):
        rows = [(scl_set if i is None else scl_beside.at[i])[j].astype(jnp.float32) for j in range(3)]
        scl[block, 0] = rows[0] if i is None else kept(has_side[i], rows[0])
        for j in range(2):
            scl[block, 1 + j] = kept(both(i, j), rows[1 + j])

    def smooth(k):
        wait_around(sem_halo.at[k], halo_units)
        for i in range(2):
            for e in range(2):
                for m in range(tip.shape[3]):
                    pair = corner[k, i, e, m].astype(jnp.int32).astype(jnp.float32)
                    corner_f32[i, e, pl.ds(2 * m, 2)] = pair.reshape(2, 8, 128)
        for s in range(size):
            at = k * size + s
            for block, i in ((0, 0), (1, None), (2, 1)):
                scales = [scl[block, j, pl.ds(at, 1)] for j in range(3)]
                q = (box[at] if i is None else beside[i, at]).astype(jnp.int32).astype(jnp.float32) * scales[0]
                if i is None:
                    tiles = [got_edge[j, at].astype(jnp.int32).astype(jnp.float32) * scales[1 + j] for j in range(2)]
                    halo = dict(enumerate(unpack_edges(*tiles)))
                else:
                    halo = unpack_tips(i, *[corner_f32[i, j, s] * scales[1 + j] for j in range(2)])
                for a in range(4):
                    slab[s, 4 * block + a, 0:16] = q[16 * a:16 * a + 16]
                    if a in halo:
                        slab[s, 4 * block + a, 16:24] = halo[a]
        for it in range(ITERS):
            for s in range(size):
                at = k * size + s
                src = slab.at[s] if it == 0 else cur.at[(it - 1) % 2, s]
                below, v = src[it], src[it + 1]
                from_layer = wts[at, it, 0]
                for a in range(1 + it, 11 - it):
                    rows = 16 if it == ITERS - 1 or a in (1 + it, 10 - it) else ZROWS
                    above = src[a + 1]
                    to_layer, to_row, to_column, inverse = (wts[at, a, f] for f in range(4))
                    acc = slab[s, a] + from_layer * below + to_layer * above
                    acc = acc + (pltpu.roll(to_row * v, 1, 0) + to_row * pltpu.roll(v, ZROWS - 1, 0))
                    v_rows, to_rows = v[0:rows], to_column[0:rows]
                    acc = acc[0:rows] + (pltpu.roll(to_rows * v_rows, 1, 1) + to_rows * pltpu.roll(v_rows, 127, 1))
                    acc = acc * inverse[0:rows]
                    if it == ITERS - 1:
                        res[at, a - 4] = acc
                    else:
                        cur[it % 2, s, a, 0:rows] = acc
                    from_layer, below, v = to_layer, v, above

    each(count, smooth)
    wait_around(sem_out, all_units)


def local(old_state, owners, diffusivity):
    species = diffusivity.shape[0]
    size = 3 if species % 3 == 0 else 1
    count = species // size
    pairs, padded = (size + 1) // 2, (species + 15) // 16 * 16
    units = 18 * species + 3 * padded // 8 + padded + 14 * species + count * (10 * size + 4 * pairs)
    i16, i32, bf16, f32 = jnp.int16, jnp.int32, jnp.bfloat16, jnp.float32
    dma = pltpu.SemaphoreType.DMA
    halves = pltpu.VMEM((2, species, 32, 128), i16)
    scratch = [
        pltpu.SMEM(owners.shape, i32),
        pltpu.VMEM(old_state.shape, f32),
        halves, halves, halves, halves, halves,
        pltpu.VMEM((2, 2, species, 32, 128), i16),
        halves,
        pltpu.VMEM((species, 64, 128), i16),
        pltpu.VMEM((2, species, 64, 128), i16),
        pltpu.VMEM((2, species, 16, 128), i16),
        pltpu.VMEM((2, species, 16, 128), i16),
        pltpu.VMEM((2, 2, 2 * pairs, 8, 128), i32),
        pltpu.VMEM((count, 2, 2, pairs, 16, 128), i16),
        pltpu.VMEM((count, 2, 2, pairs, 16, 128), i16),
        pltpu.VMEM((2, 2, 2 * pairs, 8, 128), f32),
        pltpu.VMEM((4, padded, 128), f32),
        pltpu.VMEM((3, padded, 128), bf16),
        pltpu.VMEM((4, padded, 128), bf16),
        pltpu.VMEM((3, padded, 128), bf16),
        pltpu.VMEM((2, 3, padded, 128), bf16),
        pltpu.VMEM((3, 3, padded, 128), f32),
        pltpu.VMEM((species, 4, 16, 128), bf16),
        pltpu.VMEM((2, species, 16, 128), bf16),
        pltpu.VMEM((2, species, 4, 16, 128), bf16),
        pltpu.VMEM((2, species, 16, 128), bf16),
        pltpu.VMEM((2, 2, species, 16, 128), bf16),
        pltpu.VMEM((size, 12, ZROWS, 128), f32),
        pltpu.VMEM((size, 12, ZROWS, 128), f32),
        pltpu.VMEM((2, size, 12, ZROWS, 128), f32),
        pltpu.VMEM((species, 11, 4, ZROWS, 128), f32),
        pltpu.VMEM((8 * units, 128), f32),
        dma((3,)), dma(()), dma((count,)), dma((count,)), dma((count,)), dma((2,)), dma((2,)),
    ]
    old_state, owners, diffusivity = (
        pltpu.with_memory_space_constraint(v, pltpu.HBM) for v in (old_state, owners, diffusivity)
    )
    return pl.pallas_call(
        kernel,
        out_shape=pltpu.VMEM(diffusivity.shape, f32),
        in_specs=[pl.BlockSpec(memory_space=pltpu.HBM)] * 3,
        out_specs=pl.BlockSpec(memory_space=pltpu.VMEM),
        scratch_shapes=scratch,
        name="regrid_smooth",
        compiler_params=pltpu.CompilerParams(collective_id=0, has_side_effects=True, vmem_limit_bytes=40 * 2**20),
    )(owners, old_state, diffusivity)


def solution(mesh):
    placed = (
        P(None, None, "group", "box", None),
        P("group", None, None),
        P(None, "group", "box", None),
    )
    return jax.shard_map(
        local, mesh=mesh, in_specs=placed, out_specs=P(None, "group", "box", None), check_vma=False
    )
```
